256 devices in a mesh: inst: 32 (over y, z_hi, core), tp: 8 (over x, z_lo).
Axes of the slice: x: 4, y: 4, z: 8 (z_hi: 4, z_lo: 2; z = z_hi * 2 + z_lo), core: 2. Of those that a mesh axis runs over, the one named last changes fastest.
Arguments:
- queries: bfloat16 [8192, 8192], P('inst', 'tp'), may hold values from -160 to 160
- key_values: bfloat16 [8192, 2048], P('inst', 'tp'), may hold values from -8 to 8
- out_weight: bfloat16 [8192, 4096], P('tp'), may hold values from -0.0625 to 0.0625
- prompt_of: int32 [32], replicated, may hold values from 0 to 7, as said below
- cycle_rank: int32 [32], replicated, may hold values from 0 to 6, as said below
- span_len: int32 [32], replicated, may hold values from 129 to 256, as said below
- cache_slot: int32 [64], replicated, may hold values from 0 to 63, as said below
Outputs:
- mixed: bfloat16 [8192, 4096], P('inst', 'tp')
- decode_cache: bfloat16 [64, 128, 2048], P('inst', None, 'tp')
The draws below stay inside these ranges and needn't reach their ends.
Inputs may be any that keep to these rules, and one draw needn't show every extreme that they name: `prompt_of`: every prompt number below 8 is served by one to seven instances. `cycle_rank`: the instances of one prompt hold the ranks 0, 1, 2 and so on, each once; some prompt has seven instances. `span_len`: some instance is full in every draw. `cache_slot`: A permutation of all cache slots. Slot s belongs to instance s // 2.
All inputs are finite; a program needn't handle non-finite values.
Results may differ from the reference program's by a relative error of at most 0.017.
Values may be sent and summed in bfloat16 or wider, within the bound.
A program may use at most 192 MiB of HBM per device.

```python
import math
import jax
import jax.numpy as jnp
from jax import lax

D = 4096
HQ = 64
KVH = 8
HD = 128
SPAN = 256
CACHE_BLOCKS = 2
TOKENS = 8192
CYCLES = 8
N_TP = 8


def cycle_layout(key):
    count = TOKENS // SPAN
    pairs = CYCLES // 2
    shift = jax.random.randint(jax.random.fold_in(key, 11), (pairs,), -3, 4).astype(jnp.int32).at[0].set(3)
    sizes = jnp.stack([4 + shift, 4 - shift], axis=1).reshape(CYCLES).astype(jnp.int32)
    ends = jnp.cumsum(sizes).astype(jnp.int32)
    starts = (ends - sizes).astype(jnp.int32)
    place = jnp.arange(count, dtype=jnp.int32)
    cycle_id = jnp.sum(ends[None, :] <= place[:, None], axis=1).astype(jnp.int32)
    match = cycle_id[:, None] == jnp.arange(CYCLES, dtype=jnp.int32)[None, :]
    start = jnp.sum(jnp.where(match, starts[None, :], 0), axis=1).astype(jnp.int32)
    relabel = jax.random.permutation(jax.random.fold_in(key, 14), CYCLES).astype(jnp.int32)
    label = jnp.sum(jnp.where(match, relabel[None, :], 0), axis=1).astype(jnp.int32)
    order = jax.random.permutation(jax.random.fold_in(key, 12), count)
    prompt_of = jnp.zeros((count,), jnp.int32).at[order].set(label)
    cycle_rank = jnp.zeros((count,), jnp.int32).at[order].set(place - start)
    shortfall = jax.random.randint(jax.random.fold_in(key, 13), (count,), 0, SPAN // 2)
    span_len = (SPAN - shortfall).astype(jnp.int32).at[order[0]].set(SPAN)
    return (prompt_of, cycle_rank, span_len)


def draw_prompt_of(key, part):
    shared = cycle_layout(key)
    return shared[0]


def draw_cycle_rank(key, part):
    shared = cycle_layout(key)
    return shared[1]


def draw_span_len(key, part):
    shared = cycle_layout(key)
    return shared[2]


def draw_cache_slot(key, part):
    key = jax.random.fold_in(key, 4)
    count = TOKENS // SPAN
    dests = jax.random.permutation(jax.random.fold_in(key, 1), count).astype(jnp.int32)
    sources = jax.random.permutation(jax.random.fold_in(key, 2), count)
    place = jnp.arange(count, dtype=jnp.int32)
    mode = place % 4
    here = dests[place]
    after = dests[(place + 1) % count]
    before = dests[(place + count - 1) % count]
    first = jnp.where(mode < 2, 2 * here, jnp.where(mode == 2, 2 * here, 2 * before + 1))
    second = jnp.where(mode < 2, 2 * here + 1, jnp.where(mode == 2, 2 * after, 2 * here + 1))
    pairs = jnp.stack([first, second], axis=1).astype(jnp.int32)
    return jnp.zeros((count, 2), jnp.int32).at[sources].set(pairs).reshape(count * 2)


def shared_keys(key, tie):
    base = jnp.clip(jax.random.normal(key, (TOKENS, KVH, HD), jnp.float32), -6.0, 6.0)
    noise = jnp.clip(jax.random.normal(jax.random.fold_in(key, 99), (TOKENS, KVH, HD), jnp.float32), -3.0, 3.0)
    rows = jnp.arange(TOKENS)
    pulled = jnp.where((rows % 32 == 30)[:, None, None], tie, 0.0)
    following = jnp.roll(base, -1, axis=0)
    return base + pulled * (following + 0.15 * noise - base)


def draw_key_values(key, part):
    keys = shared_keys(key, 0.0)
    key = jax.random.fold_in(key, 5)
    values = jnp.clip(jax.random.normal(key, (TOKENS, KVH, HD), jnp.float32), -6.0, 6.0)
    return jnp.stack([keys, values], axis=2).reshape(TOKENS, KVH * 2 * HD).astype(jnp.bfloat16)


def draw_queries(key, part):
    key = jax.random.fold_in(key, 7)
    base = jnp.clip(jax.random.normal(key, (TOKENS, HQ, HD), jnp.float32), -6.0, 6.0)
    return base.reshape(TOKENS, HQ * HD).astype(jnp.bfloat16)


def shard_levels(own_key, shape, cuts, smallest, top_value):
    level = 1.0
    for axis_at, parts in cuts:
        heights = jax.random.uniform(jax.random.fold_in(jax.random.fold_in(own_key, 6), axis_at), (parts,), jnp.float32, smallest / len(cuts), top_value / len(cuts))
        level = level * jnp.repeat(jnp.exp(heights), shape[axis_at] // parts).reshape((-1,) + (1,) * (len(shape) - 1 - axis_at))
    return level


def centred(stream_key, dims, spread, bound, cuts=(), held_as=jnp.bfloat16):
    values = jax.random.normal(stream_key, dims, jnp.float32) * spread
    if len(cuts) > 0:
        values = shard_levels(stream_key, dims, cuts, -0.22, 0.18) * values
    return jnp.clip(values, min=-bound, max=bound).astype(held_as)


def setup_inputs(seed: int = 0) -> dict:
    key_of = jax.random.split(jax.random.key(seed), 8)
    queries = draw_queries(jax.random.fold_in(key_of[7], 71), 0)
    key_values = draw_key_values(jax.random.fold_in(key_of[7], 71), 0)
    out_weight = centred(key_of[2], (HQ * HD, D), (HQ * HD) ** -0.5, 0.0625, ((0, 8),))
    prompt_of = draw_prompt_of(jax.random.fold_in(key_of[7], 71), 0)
    cycle_rank = draw_cycle_rank(jax.random.fold_in(key_of[7], 71), 0)
    span_len = draw_span_len(jax.random.fold_in(key_of[7], 71), 0)
    cache_slot = draw_cache_slot(jax.random.fold_in(key_of[7], 71), 0)
    return dict(queries=queries, key_values=key_values, out_weight=out_weight, prompt_of=prompt_of, cycle_rank=cycle_rank, span_len=span_len, cache_slot=cache_slot)


NEG_LARGE = -1e+30

def earlier_offsets(prompt_of, cycle_rank, span_len):
    same_cycle = prompt_of[None, :] == prompt_of[:, None]
    before = cycle_rank[None, :] < cycle_rank[:, None]
    return lax.optimization_barrier(jnp.sum(jnp.where(same_cycle & before, span_len[None, :], 0), axis=1)).astype(jnp.int32)

def rounded(values):
    narrow = lax.optimization_barrier(values.astype(jnp.bfloat16))
    return narrow.astype(jnp.float32)

def reference(queries, key_values, out_weight, prompt_of, cycle_rank, span_len, cache_slot):
    devices = TOKENS // SPAN
    group = HQ // KVH
    scale = 1.0 / math.sqrt(HD)
    offsets = earlier_offsets(prompt_of, cycle_rank, span_len)
    slots = jnp.arange(TOKENS, dtype=jnp.int32)
    owner = (slots // SPAN).astype(jnp.int32)
    inside = (slots % SPAN).astype(jnp.int32)
    live = inside < span_len[owner]
    position = offsets[owner] + inside
    prompt = prompt_of[owner]
    split = key_values.reshape(TOKENS, KVH, 2, HD)
    keys_all = split[:, :, 0].transpose(1, 0, 2)
    values_all = split[:, :, 1].transpose(1, 0, 2)
    grouped = queries.reshape(devices, SPAN, KVH, group, HD).transpose(0, 2, 1, 3, 4)

    def one_block(block_args):
        query_block, query_live, query_pos, query_prompt = block_args
        allowed = query_live[:, None] & live[None, :] & (prompt[None, :] == query_prompt[:, None]) & (position[None, :] <= query_pos[:, None])

        def one_head(head_args):
            query_head, key_head, value_head = head_args
            scores = jnp.einsum('qgd,kd->gqk', query_head.astype(jnp.float32), key_head.astype(jnp.float32)) * scale
            scores = jnp.where(allowed[None], scores, NEG_LARGE)
            largest = lax.optimization_barrier(jnp.max(scores, axis=-1, keepdims=True))
            expos = jnp.where(allowed[None], jnp.exp(scores - largest), 0.0)
            total = lax.optimization_barrier(jnp.sum(expos, axis=-1))
            weights = expos.astype(jnp.bfloat16)
            numer = jnp.einsum('gqk,kd->gqd', weights.astype(jnp.float32), value_head.astype(jnp.float32))
            return numer / jnp.where(total > 0.0, total, 1.0)[..., None]
        heads = lax.map(one_head, (query_block, keys_all, values_all))
        return heads.transpose(2, 0, 1, 3).reshape(SPAN, HQ * HD).astype(jnp.bfloat16)
    attended = lax.map(one_block, (grouped, live.reshape(devices, SPAN), position.reshape(devices, SPAN), prompt.reshape(devices, SPAN)))
    attended = attended.reshape(TOKENS, HQ * HD)
    column_group = HQ * HD // N_TP

    def add_group(total, index):
        part_rows = lax.dynamic_slice_in_dim(attended, index * column_group, column_group, 1)
        part_weight = lax.dynamic_slice_in_dim(out_weight, index * column_group, column_group, 0)
        product = jnp.dot(part_rows, part_weight, preferred_element_type=jnp.float32)
        return (total + rounded(product), None)
    total, unused = lax.scan(add_group, jnp.zeros((TOKENS, D), jnp.float32), jnp.arange(N_TP, dtype=jnp.int32))
    mixed = total.astype(jnp.bfloat16)
    blocks = key_values.reshape(devices * CACHE_BLOCKS, SPAN // CACHE_BLOCKS, KVH * 2 * HD)
    decode_cache = jnp.zeros_like(blocks).at[cache_slot].set(blocks)
    return (mixed, decode_cache)
```

```python
import functools
import math

import jax
import jax.numpy as jnp
from jax import lax
from jax.experimental import pallas as pl
from jax.experimental.pallas import tpu as pltpu
from jax.sharding import PartitionSpec as P

HD = 128
SPAN = 256
HEADS = 8
EARLIER = 6
KEYS = (EARLIER + 1) * SPAN
CHUNK = 512
ZROWS = 160
XROWS = SPAN - ZROWS
NEG = -1e30
MESH = pl.DeviceIdType.MESH
COPIES = 96


def kernel(
    q_hbm, kv_hbm, w_hbm, prompt_hbm, rank_hbm, len_hbm, slot_hbm,
    mixed_hbm, cache_hbm,
    qbuf, kbuf, vbuf, wbuf, kcat, vcat, bias, probs, totals, att,
    zsend, zrecv, own1, xsend, xrecv, x2send, x2recv, own2, z2send, z2recv,
    mixbuf, cachebuf,
    prompt, rank, length, slot,
    local_sem, send_sem, recv_sem,
):
    me = lax.axis_index("inst")
    tp = lax.axis_index("tp")
    y, zh, core = me // 8, (me // 2) % 4, me % 2
    x, zl = tp // 2, tp % 2

    def inst_at(dy, dz, dc):
        return (((y + dy) % 4) * 4 + (zh + dz) % 4) * 2 + (core + dc) % 2

    def tp_at(dx, dz):
        return ((x + dx) % 4) * 2 + (zl + dz) % 2

    z_up, z_down = (inst_at(0, 1, 0), tp), (inst_at(0, 3, 0), tp)
    y_up, y_down = (inst_at(1, 0, 0), tp), (inst_at(3, 0, 0), tp)
    sibling = (inst_at(0, 0, 1), tp)
    z_pair = (me, tp_at(0, 1))
    x_peer = {dx: (me, tp_at(dx, 0)) for dx in (1, 2, 3)}

    n_local = [0]

    def local(src, dst):
        copy = pltpu.make_async_copy(src, dst, local_sem.at[n_local[0]])
        n_local[0] += 1
        copy.start()
        return copy

    own_k = local(kv_hbm.at[:, pl.ds(0, HD)], kbuf.at[0])
    own_v = local(kv_hbm.at[:, pl.ds(HD, HD)], vbuf.at[0])
    tables = [
        local(src, dst)
        for src, dst in (
            (prompt_hbm, prompt), (rank_hbm, rank), (len_hbm, length), (slot_hbm, slot)
        )
    ]
    q_copy = local(q_hbm, qbuf)

    barrier = pltpu.get_barrier_semaphore()
    friends = [z_up, z_down, y_up, y_down, sibling, z_pair] + list(x_peer.values())
    for friend in friends:
        pl.semaphore_signal(barrier, inc=1, device_id=friend, device_id_type=MESH)
    w_copies = {}
    for dz in (1, 0):
        for dx in (2, 1, 3, 0):
            columns = pl.ds(pl.multiple_of(tp_at(dx, dz) * CHUNK, CHUNK), CHUNK)
            w_copies[dx, dz] = local(w_hbm.at[:, columns], wbuf.at[dx * 2 + dz])
    pl.semaphore_wait(barrier, len(friends))

    sent = []

    def send(src, dst, device):
        index = len(sent)
        copy = pltpu.make_async_remote_copy(
            src_ref=src, dst_ref=dst, send_sem=send_sem.at[index], recv_sem=recv_sem.at[index],
            device_id=device, device_id_type=MESH,
        )
        copy.start()
        sent.append(copy)
        return copy

    own_k.wait()
    own_v.wait()
    z_k = {3: send(kbuf.at[0], kbuf.at[3], z_up), 1: send(kbuf.at[0], kbuf.at[1], z_down)}
    yu, yd = {}, {}

    def along_y(name, buf, dz):
        yu[name, dz] = send(buf.at[dz], buf.at[12 + dz], y_up)
        yd[name, dz] = send(buf.at[dz], buf.at[4 + dz], y_down)

    far = {}

    def onward(name, buf, dz):
        if dz < 2:
            yu[name, dz].wait_recv()
            far[name, dz] = send(buf.at[12 + dz], buf.at[8 + dz], y_up)
        else:
            yd[name, dz].wait_recv()
            far[name, dz] = send(buf.at[4 + dz], buf.at[8 + dz], y_down)

    def rest_near(name, dz):
        (yd if dz < 2 else yu)[name, dz].wait_recv()

    across = {}

    def to_sibling(name, buf, start, count):
        across[name, start] = send(
            buf.at[pl.ds(start, count)], buf.at[pl.ds(16 + start, count)], sibling
        )

    along_y("k", kbuf, 0)
    z_v = {3: send(vbuf.at[0], vbuf.at[3], z_up), 1: send(vbuf.at[0], vbuf.at[1], z_down)}
    along_y("v", vbuf, 0)
    to_sibling("k", kbuf, 0, 1)
    to_sibling("v", vbuf, 0, 1)

    z_k[3].wait_recv()
    z_k[2] = send(kbuf.at[3], kbuf.at[2], z_up)
    along_y("k", kbuf, 3)
    z_k[1].wait_recv()
    along_y("k", kbuf, 1)

    for copy in tables:
        copy.wait()
    my_prompt, my_rank, my_len = prompt[me], rank[me], length[me]

    who, live = [me] * EARLIER, [jnp.int32(0)] * EARLIER
    for j in range(32):
        same, its_rank, its_len = prompt[j] == my_prompt, rank[j], length[j]
        for s in range(EARLIER):
            hit = same & (its_rank == s) & (s < my_rank)
            who[s] = jnp.where(hit, j, who[s])
            live[s] = jnp.where(hit, its_len, live[s])
    block_of = [jnp.int32(0)] * 2
    for b in range(64):
        for s in range(2):
            block_of[s] = jnp.where(slot[b] == 2 * me + s, b, block_of[s])

    def place(j):
        dy = ((j >> 3) + 4 - y) & 3
        dz = (((j >> 1) & 3) + 4 - zh) & 3
        dc = ((j & 1) + 2 - core) & 1
        return dc * 16 + dy * 4 + dz

    lane = lax.broadcasted_iota(jnp.int32, (1, SPAN), 1)
    for s in range(EARLIER):
        bias[:, s * SPAN:(s + 1) * SPAN] = jnp.where(lane < live[s], 0.0, NEG)

    z_k[2].wait_recv()
    along_y("k", kbuf, 2)
    to_sibling("k", kbuf, 1, 3)
    z_v[3].wait_recv()
    z_v[1].wait_recv()
    z_v[2] = send(vbuf.at[1], vbuf.at[2], z_down)
    onward("k", kbuf, 0)
    along_y("v", vbuf, 3)
    along_y("v", vbuf, 1)
    onward("k", kbuf, 3)
    onward("k", kbuf, 1)
    onward("k", kbuf, 2)
    z_v[2].wait_recv()
    along_y("v", vbuf, 2)
    to_sibling("v", vbuf, 1, 3)
    for dz in range(4):
        rest_near("k", dz)
    to_sibling("k", kbuf, 4, 4)
    to_sibling("k", kbuf, 12, 4)
    onward("v", vbuf, 0)
    for dz in range(4):
        far["k", dz].wait_recv()
    to_sibling("k", kbuf, 8, 4)
    for start in (0, 1, 4, 12, 8):
        across["k", start].wait_recv()

    q_copy.wait()
    for s in range(EARLIER):
        kcat[s * SPAN:(s + 1) * SPAN, :] = kbuf[place(who[s])]
    kcat[EARLIER * SPAN:, :] = kbuf[0]
    rows = 128
    factor = math.log2(math.e) / math.sqrt(HD)

    def weigh(head):
        @pl.loop(0, SPAN // rows)
        def _(part):
            start = pl.multiple_of(part * rows, rows)
            scores = lax.dot_general(
                qbuf[pl.ds(start, rows), head * HD:(head + 1) * HD], kcat[...],
                (((1,), (1,)), ((), ())), preferred_element_type=jnp.float32,
            )
            earlier = scores[:, :EARLIER * SPAN] + bias[...]
            row = lax.broadcasted_iota(jnp.int32, (rows, SPAN), 0) + start
            column = lax.broadcasted_iota(jnp.int32, (rows, SPAN), 1)
            here = jnp.where(column <= row, scores[:, EARLIER * SPAN:], NEG)
            top = jnp.maximum(
                jnp.max(earlier, axis=1, keepdims=True), jnp.max(here, axis=1, keepdims=True)
            )
            earlier = jnp.exp2((earlier - top) * factor)
            here = jnp.exp2((here - top) * factor)
            total = jnp.sum(earlier, axis=1, keepdims=True) + jnp.sum(here, axis=1, keepdims=True)
            its_row = lax.broadcasted_iota(jnp.int32, (rows, 1), 0) + start
            inverse = jnp.where(its_row < my_len, 1.0 / total, 0.0)
            probs[head, pl.ds(start, rows), :EARLIER * SPAN] = earlier.astype(jnp.bfloat16)
            probs[head, pl.ds(start, rows), EARLIER * SPAN:] = here.astype(jnp.bfloat16)
            totals[head, pl.ds(start, rows), :] = jnp.broadcast_to(inverse, (rows, HD))

    def near_done():
        for dz in range(4):
            rest_near("v", dz)
        to_sibling("v", vbuf, 4, 4)
        to_sibling("v", vbuf, 12, 4)

    def far_done():
        for dz in range(4):
            far["v", dz].wait_recv()
        to_sibling("v", vbuf, 8, 4)

    between = {
        1: lambda: onward("v", vbuf, 3),
        2: lambda: onward("v", vbuf, 1),
        4: lambda: onward("v", vbuf, 2),
        5: near_done,
        7: far_done,
    }
    for head in range(HEADS):
        weigh(head)
        if head in between:
            between[head]()
    for start in (0, 1, 4, 12, 8):
        across["v", start].wait_recv()

    for s in range(EARLIER):
        vcat[s * SPAN:(s + 1) * SPAN, :] = vbuf[place(who[s])]
    vcat[EARLIER * SPAN:, :] = vbuf[0]
    for head in range(HEADS):
        numer = jnp.dot(probs[head], vcat[...], preferred_element_type=jnp.float32)
        att[:, head * HD:(head + 1) * HD] = (numer * totals[head]).astype(jnp.bfloat16)

    z1, x2 = {}, {}
    for dx in (2, 1, 3, 0):
        w_copies[dx, 1].wait()
        term = jnp.dot(att[...], wbuf[dx * 2 + 1], preferred_element_type=jnp.float32)
        zsend[dx] = term[:ZROWS].astype(jnp.bfloat16)
        z1[dx] = send(zsend.at[dx], zrecv.at[dx], z_pair)
        if dx:
            x2send[dx - 1, 1] = term[ZROWS:].astype(jnp.bfloat16)
            x2[dx, 1] = send(x2send.at[dx - 1, 1], x2recv.at[dx - 1, 1], x_peer[dx])
        else:
            own2[1] = term[ZROWS:]
    for dx in (2, 1, 3, 0):
        w_copies[dx, 0].wait()
        term = jnp.dot(att[...], wbuf[dx * 2], preferred_element_type=jnp.float32)
        own1[dx] = term[:ZROWS]
        if dx:
            x2send[dx - 1, 0] = term[ZROWS:].astype(jnp.bfloat16)
            x2[dx, 0] = send(x2send.at[dx - 1, 0], x2recv.at[dx - 1, 0], x_peer[dx])
        else:
            own2[0] = term[ZROWS:]

    x1 = {}

    def pass_on(dx):
        z1[dx].wait_recv()
        xsend[dx - 1] = (own1[dx] + zrecv[dx].astype(jnp.float32)).astype(jnp.bfloat16)
        x1[dx] = send(xsend.at[dx - 1], xrecv.at[dx - 1], x_peer[dx])

    pass_on(2)
    for dx in (1, 3, 2):
        x2[dx, 1].wait_recv()
    total = own2[1]
    for k in range(3):
        total = total + x2recv[k, 1].astype(jnp.float32)
    z2send[...] = total.astype(jnp.bfloat16)
    z2 = send(z2send, z2recv, z_pair)
    pass_on(1)

    for s in range(2):
        its, second = place(block_of[s] >> 1), (block_of[s] & 1) == 1
        for buf, at in ((kbuf, 0), (vbuf, HD)):
            block = buf[its]
            cachebuf[s, :, at:at + HD] = jnp.where(second, block[SPAN // 2:], block[:SPAN // 2])
    cache_copy = local(cachebuf, cache_hbm)
    pass_on(3)

    for dx in (1, 3, 2):
        x2[dx, 0].wait_recv()
    z2.wait_recv()
    total = own2[0] + z2recv[...].astype(jnp.float32)
    for k in range(3):
        total = total + x2recv[k, 0].astype(jnp.float32)
    mixbuf[ZROWS:, :] = total.astype(jnp.bfloat16)
    out_low = local(mixbuf.at[pl.ds(ZROWS, XROWS)], mixed_hbm.at[pl.ds(ZROWS, XROWS)])

    z1[0].wait_recv()
    for dx in (2, 1, 3):
        x1[dx].wait_recv()
    total = own1[0] + zrecv[0].astype(jnp.float32)
    for k in range(3):
        total = total + xrecv[k].astype(jnp.float32)
    mixbuf[:ZROWS, :] = total.astype(jnp.bfloat16)
    out_high = local(mixbuf.at[pl.ds(0, ZROWS)], mixed_hbm.at[pl.ds(0, ZROWS)])

    for copy in sent:
        copy.wait_send()
    cache_copy.wait()
    out_low.wait()
    out_high.wait()


def on_device(queries, key_values, out_weight, prompt_of, cycle_rank, span_len, cache_slot):
    bf16, f32 = jnp.bfloat16, jnp.float32
    width = HEADS * HD
    vmem = pltpu.VMEM
    return pl.pallas_call(
        kernel,
        out_shape=(
            jax.ShapeDtypeStruct((SPAN, CHUNK), bf16),
            jax.ShapeDtypeStruct((2, SPAN // 2, 2 * HD), bf16),
        ),
        in_specs=[pl.BlockSpec(memory_space=pl.ANY)] * 7,
        out_specs=[pl.BlockSpec(memory_space=pl.ANY)] * 2,
        scratch_shapes=[
            vmem((SPAN, width), bf16),
            vmem((32, SPAN, HD), bf16),
            vmem((32, SPAN, HD), bf16),
            vmem((8, width, CHUNK), bf16),
            vmem((KEYS, HD), bf16),
            vmem((KEYS, HD), bf16),
            vmem((1, EARLIER * SPAN), f32),
            vmem((HEADS, SPAN, KEYS), bf16),
            vmem((HEADS, SPAN, HD), f32),
            vmem((SPAN, width), bf16),
            vmem((4, ZROWS, CHUNK), bf16),
            vmem((4, ZROWS, CHUNK), bf16),
            vmem((4, ZROWS, CHUNK), f32),
            vmem((3, ZROWS, CHUNK), bf16),
            vmem((3, ZROWS, CHUNK), bf16),
            vmem((3, 2, XROWS, CHUNK), bf16),
            vmem((3, 2, XROWS, CHUNK), bf16),
            vmem((2, XROWS, CHUNK), f32),
            vmem((XROWS, CHUNK), bf16),
            vmem((XROWS, CHUNK), bf16),
            vmem((SPAN, CHUNK), bf16),
            vmem((2, SPAN // 2, 2 * HD), bf16),
            pltpu.SMEM((32,), jnp.int32),
            pltpu.SMEM((32,), jnp.int32),
            pltpu.SMEM((32,), jnp.int32),
            pltpu.SMEM((64,), jnp.int32),
            pltpu.SemaphoreType.DMA((24,)),
            pltpu.SemaphoreType.DMA((COPIES,)),
            pltpu.SemaphoreType.DMA((COPIES,)),
        ],
        compiler_params=pltpu.CompilerParams(
            collective_id=0, has_side_effects=True, vmem_limit_bytes=56 * 1024 * 1024
        ),
        cost_estimate=pl.CostEstimate(
            flops=4 * SPAN * HEADS * KEYS * HD + 2 * SPAN * width * 4096,
            bytes_accessed=10 * 1024 * 1024,
            transcendentals=HEADS * SPAN * KEYS,
        ),
    )(queries, key_values, out_weight, prompt_of, cycle_rank, span_len, cache_slot)


def solution(mesh):
    placed = (P("inst", "tp"), P("inst", "tp"), P("tp", None), P(), P(), P(), P())
    return jax.shard_map(
        on_device,
        mesh=mesh,
        in_specs=placed,
        out_specs=(P("inst", "tp"), P("inst", None, "tp")),
        check_vma=False,
    )
```

```python
import functools
import math

import jax
import jax.numpy as jnp
from jax import lax
from jax.experimental import pallas as pl
from jax.experimental.pallas import tpu as pltpu
from jax.sharding import PartitionSpec as P

HD = 128
SPAN = 256
HEADS = 8
EARLIER = 6
KEYS = (EARLIER + 1) * SPAN
CHUNK = 512
ZROWS = 160
XROWS = SPAN - ZROWS
NEG = -1e30
MESH = pl.DeviceIdType.MESH
COPIES = 96

PLAN = (
    "+zk3", "+zk1", "+k0u", "+k0d", "+v0d", "?k0u", "+v0u", "+zv1", "?zk3", "+k3d", "?zk1", "+k1u",
    "+zk2", "?v0d", "+fk0", "?k0d", "?v0u", "+k1d", "?zv1", "+v1d", "+k3u", "+zv2", "+xv0", "?k1u",
    "+zv3", "?zk2", "+k2d", "+fk1", "+xk0", "+xk1", "?xk1", "?k3d", "+fk3", "?k1d", "+k2u", "?k3u",
    "?v1d", "?k2d", "+fk2", "?zv2", "+v2u", "+xk4", "?xk0", "?xv0", "?zv3", "+xv1", "+v3u", "?xk4",
    "?k2u", "+v3d", "?fk3", "+fv1", "?fk0", "?fk1", "+xk12", "?xv1", "+xk8", "?fk2", "+xk10",
    "+v1u", "?xk8", "+v2d", "+fv0", "?v2u", "?xk12", "+fv2", "?xk10", "#", "?v3u", "#", "+fv3",
    "#", "#", "?v1u", "+xv12", "#", "?fv2", "#", "?fv1", "?v3d", "?fv0", "+xv8", "?fv3", "?v2d",
    "+xv4", "?xv12", "+xv10", "#", "#", "?xv10", "?xv8", "?xv4",
)


def kernel(
    q_hbm, kv_hbm, w_hbm, prompt_hbm, rank_hbm, len_hbm, slot_hbm,
    mixed, cache,
    qbuf, kbuf, vbuf, wbuf, kcat, vcat, bias, probs, totals, att,
    zsend, zrecv, own1, xsend, xrecv, x2send, x2recv, own2, z2send, z2recv,
    prompt, rank, length, slot,
    local_sem, send_sem, recv_sem,
):
    me = lax.axis_index("inst")
    tp = lax.axis_index("tp")
    y, zh, core = me // 8, (me // 2) % 4, me % 2
    x, zl = tp // 2, tp % 2

    def inst_at(dy, dz, dc):
        return (((y + dy) % 4) * 4 + (zh + dz) % 4) * 2 + (core + dc) % 2

    def tp_at(dx, dz):
        return ((x + dx) % 4) * 2 + (zl + dz) % 2

    z_up, z_down = (inst_at(0, 1, 0), tp), (inst_at(0, 3, 0), tp)
    y_up, y_down = (inst_at(1, 0, 0), tp), (inst_at(3, 0, 0), tp)
    sibling = (inst_at(0, 0, 1), tp)
    z_pair = (me, tp_at(0, 1))
    x_peer = {dx: (me, tp_at(dx, 0)) for dx in (1, 2, 3)}

    n_local = [0]

    def local(src, dst):
        copy = pltpu.make_async_copy(src, dst, local_sem.at[n_local[0]])
        n_local[0] += 1
        copy.start()
        return copy

    own_k = local(kv_hbm.at[:, pl.ds(0, HD)], kbuf.at[0])
    own_v = local(kv_hbm.at[:, pl.ds(HD, HD)], vbuf.at[0])
    tables = [
        local(src, dst)
        for src, dst in (
            (prompt_hbm, prompt), (rank_hbm, rank), (len_hbm, length), (slot_hbm, slot)
        )
    ]
    q_copy = local(q_hbm, qbuf)

    barrier = pltpu.get_barrier_semaphore()
    friends = [z_up, z_down, y_up, y_down, sibling, z_pair] + list(x_peer.values())
    for friend in friends:
        pl.semaphore_signal(barrier, inc=1, device_id=friend, device_id_type=MESH)
    w_copies = {}
    for dz in (1, 0):
        for dx in (2, 1, 3, 0):
            columns = pl.ds(pl.multiple_of(tp_at(dx, dz) * CHUNK, CHUNK), CHUNK)
            w_copies[dx, dz] = local(w_hbm.at[:, columns], wbuf.at[dx * 2 + dz])
    pl.semaphore_wait(barrier, len(friends))

    sent = []

    def send(src, dst, device):
        index = len(sent)
        copy = pltpu.make_async_remote_copy(
            src_ref=src, dst_ref=dst, send_sem=send_sem.at[index], recv_sem=recv_sem.at[index],
            device_id=device, device_id_type=MESH,
        )
        copy.start()
        sent.append(copy)
        return copy

    bufs = {"k": kbuf, "v": vbuf}
    copies = {}

    def start_copy(name):
        if name[0] in "zfx":
            kind, buf, slot_at = name[0], bufs[name[1]], int(name[2:])
        else:
            kind, buf, slot_at = name[2], bufs[name[0]], int(name[1])
        onward_up = (slot_at < 2) == (buf is kbuf)
        source, target, count, device = {
            "z": lambda: {
                3: (0, 3, 1, z_up),
                1: (0, 1, 1, z_down),
                2: (3, 2, 1, z_up) if buf is kbuf else (1, 2, 1, z_down),
            }[slot_at],
            "u": lambda: (slot_at, 12 + slot_at, 1, y_up),
            "d": lambda: (slot_at, 4 + slot_at, 1, y_down),
            "f": lambda: (12 + slot_at, 8 + slot_at, 1, y_up)
            if onward_up
            else (4 + slot_at, 8 + slot_at, 1, y_down),
            "x": lambda: (
                slot_at, 16 + slot_at, {0: 1, 1: 3, 4: 4, 12: 4, 8: 2, 10: 2}[slot_at], sibling
            ),
        }[kind]()
        copies[name] = send(
            buf.at[pl.ds(source, count)], buf.at[pl.ds(target, count)], device
        )

    arrived = set()

    def arrive(name):
        if name not in arrived:
            arrived.add(name)
            copies[name].wait_recv()

    own_k.wait()
    own_v.wait()
    first_head = PLAN.index("#")
    for step in PLAN[:PLAN.index("?zk3")]:
        (start_copy if step[0] == "+" else arrive)(step[1:])

    for copy in tables:
        copy.wait()
    my_prompt, my_rank, my_len = prompt[me], rank[me], length[me]
    who, live = [me] * EARLIER, [jnp.int32(0)] * EARLIER
    for j in range(32):
        same, its_rank, its_len = prompt[j] == my_prompt, rank[j], length[j]
        for s in range(EARLIER):
            hit = same & (its_rank == s) & (s < my_rank)
            who[s] = jnp.where(hit, j, who[s])
            live[s] = jnp.where(hit, its_len, live[s])
    block_of = [jnp.int32(0)] * 2
    for b in range(64):
        for s in range(2):
            block_of[s] = jnp.where(slot[b] == 2 * me + s, b, block_of[s])

    def place(j):
        dy = ((j >> 3) + 4 - y) & 3
        dz = (((j >> 1) & 3) + 4 - zh) & 3
        dc = ((j & 1) + 2 - core) & 1
        return dc * 16 + dy * 4 + dz

    lane = lax.broadcasted_iota(jnp.int32, (1, SPAN), 1)
    for s in range(EARLIER):
        bias[:, s * SPAN:(s + 1) * SPAN] = jnp.where(lane < live[s], 0.0, NEG)

    for step in PLAN[PLAN.index("?zk3"):first_head]:
        (start_copy if step[0] == "+" else arrive)(step[1:])

    q_copy.wait()
    for s in range(EARLIER):
        kcat[s * SPAN:(s + 1) * SPAN, :] = kbuf[place(who[s])]
    kcat[EARLIER * SPAN:, :] = kbuf[0]
    rows = 128
    factor = math.log2(math.e) / math.sqrt(HD)

    def weigh(head):
        @pl.loop(0, SPAN // rows)
        def _(part):
            start = pl.multiple_of(part * rows, rows)
            scores = lax.dot_general(
                qbuf[pl.ds(start, rows), head * HD:(head + 1) * HD], kcat[...],
                (((1,), (1,)), ((), ())), preferred_element_type=jnp.float32,
            )
            earlier = scores[:, :EARLIER * SPAN] + bias[...]
            row = lax.broadcasted_iota(jnp.int32, (rows, SPAN), 0) + start
            column = lax.broadcasted_iota(jnp.int32, (rows, SPAN), 1)
            here = jnp.where(column <= row, scores[:, EARLIER * SPAN:], NEG)
            top = jnp.maximum(
                jnp.max(earlier, axis=1, keepdims=True), jnp.max(here, axis=1, keepdims=True)
            )
            earlier = jnp.exp2((earlier - top) * factor)
            here = jnp.exp2((here - top) * factor)
            total = jnp.sum(earlier, axis=1, keepdims=True) + jnp.sum(here, axis=1, keepdims=True)
            its_row = lax.broadcasted_iota(jnp.int32, (rows, 1), 0) + start
            inverse = jnp.where(its_row < my_len, 1.0 / total, 0.0)
            probs[head, pl.ds(start, rows), :EARLIER * SPAN] = earlier.astype(jnp.bfloat16)
            probs[head, pl.ds(start, rows), EARLIER * SPAN:] = here.astype(jnp.bfloat16)
            totals[head, pl.ds(start, rows), :] = jnp.broadcast_to(inverse, (rows, HD))

    head = 0
    for step in PLAN[first_head:]:
        if step == "#":
            weigh(head)
            head += 1
        else:
            (start_copy if step[0] == "+" else arrive)(step[1:])
    for name in copies:
        arrive(name)

    for s in range(EARLIER):
        vcat[s * SPAN:(s + 1) * SPAN, :] = vbuf[place(who[s])]
    vcat[EARLIER * SPAN:, :] = vbuf[0]
    for head in range(HEADS):
        numer = jnp.dot(probs[head], vcat[...], preferred_element_type=jnp.float32)
        att[:, head * HD:(head + 1) * HD] = (numer * totals[head]).astype(jnp.bfloat16)

    z1, x2 = {}, {}
    for dx in (2, 1, 3, 0):
        w_copies[dx, 1].wait()
        term = jnp.dot(att[...], wbuf[dx * 2 + 1], preferred_element_type=jnp.float32)
        zsend[dx] = term[:ZROWS].astype(jnp.bfloat16)
        z1[dx] = send(zsend.at[dx], zrecv.at[dx], z_pair)
        if dx:
            x2send[dx - 1, 1] = term[ZROWS:].astype(jnp.bfloat16)
            x2[dx, 1] = send(x2send.at[dx - 1, 1], x2recv.at[dx - 1, 1], x_peer[dx])
        else:
            own2[1] = term[ZROWS:]
    for dx in (2, 1, 3, 0):
        w_copies[dx, 0].wait()
        term = jnp.dot(att[...], wbuf[dx * 2], preferred_element_type=jnp.float32)
        own1[dx] = term[:ZROWS]
        if dx:
            x2send[dx - 1, 0] = term[ZROWS:].astype(jnp.bfloat16)
            x2[dx, 0] = send(x2send.at[dx - 1, 0], x2recv.at[dx - 1, 0], x_peer[dx])
        else:
            own2[0] = term[ZROWS:]

    x1 = {}

    def pass_on(dx):
        z1[dx].wait_recv()
        xsend[dx - 1] = (own1[dx] + zrecv[dx].astype(jnp.float32)).astype(jnp.bfloat16)
        x1[dx] = send(xsend.at[dx - 1], xrecv.at[dx - 1], x_peer[dx])

    pass_on(2)
    for dx in (1, 3, 2):
        x2[dx, 1].wait_recv()
    total = own2[1]
    for k in range(3):
        total = total + x2recv[k, 1].astype(jnp.float32)
    z2send[...] = total.astype(jnp.bfloat16)
    z2 = send(z2send, z2recv, z_pair)
    pass_on(1)

    for s in range(2):
        its, second = place(block_of[s] >> 1), (block_of[s] & 1) == 1
        for buf, at in ((kbuf, 0), (vbuf, HD)):
            block = buf[its]
            cache[s, :, at:at + HD] = jnp.where(second, block[SPAN // 2:], block[:SPAN // 2])
    pass_on(3)

    for dx in (1, 3, 2):
        x2[dx, 0].wait_recv()
    z2.wait_recv()
    total = own2[0] + z2recv[...].astype(jnp.float32)
    for k in range(3):
        total = total + x2recv[k, 0].astype(jnp.float32)
    mixed[ZROWS:, :] = total.astype(jnp.bfloat16)

    z1[0].wait_recv()
    for dx in (2, 1, 3):
        x1[dx].wait_recv()
    total = own1[0] + zrecv[0].astype(jnp.float32)
    for k in range(3):
        total = total + xrecv[k].astype(jnp.float32)
    mixed[:ZROWS, :] = total.astype(jnp.bfloat16)

    for copy in sent:
        copy.wait_send()


def on_device(queries, key_values, out_weight, prompt_of, cycle_rank, span_len, cache_slot):
    bf16, f32 = jnp.bfloat16, jnp.float32
    width = HEADS * HD
    vmem = pltpu.VMEM
    return pl.pallas_call(
        kernel,
        out_shape=(
            vmem((SPAN, CHUNK), bf16),
            vmem((2, SPAN // 2, 2 * HD), bf16),
        ),
        in_specs=[pl.BlockSpec(memory_space=pl.ANY)] * 7,
        out_specs=(pl.BlockSpec(memory_space=pltpu.VMEM),) * 2,
        scratch_shapes=[
            vmem((SPAN, width), bf16),
            vmem((32, SPAN, HD), bf16),
            vmem((32, SPAN, HD), bf16),
            vmem((8, width, CHUNK), bf16),
            vmem((KEYS, HD), bf16),
            vmem((KEYS, HD), bf16),
            vmem((1, EARLIER * SPAN), f32),
            vmem((HEADS, SPAN, KEYS), bf16),
            vmem((HEADS, SPAN, HD), f32),
            vmem((SPAN, width), bf16),
            vmem((4, ZROWS, CHUNK), bf16),
            vmem((4, ZROWS, CHUNK), bf16),
            vmem((4, ZROWS, CHUNK), f32),
            vmem((3, ZROWS, CHUNK), bf16),
            vmem((3, ZROWS, CHUNK), bf16),
            vmem((3, 2, XROWS, CHUNK), bf16),
            vmem((3, 2, XROWS, CHUNK), bf16),
            vmem((2, XROWS, CHUNK), f32),
            vmem((XROWS, CHUNK), bf16),
            vmem((XROWS, CHUNK), bf16),
            pltpu.SMEM((32,), jnp.int32),
            pltpu.SMEM((32,), jnp.int32),
            pltpu.SMEM((32,), jnp.int32),
            pltpu.SMEM((64,), jnp.int32),
            pltpu.SemaphoreType.DMA((24,)),
            pltpu.SemaphoreType.DMA((COPIES,)),
            pltpu.SemaphoreType.DMA((COPIES,)),
        ],
        compiler_params=pltpu.CompilerParams(
            collective_id=0, has_side_effects=True, vmem_limit_bytes=56 * 1024 * 1024
        ),
        cost_estimate=pl.CostEstimate(
            flops=4 * SPAN * HEADS * KEYS * HD + 2 * SPAN * width * 4096,
            bytes_accessed=10 * 1024 * 1024,
            transcendentals=HEADS * SPAN * KEYS,
        ),
    )(queries, key_values, out_weight, prompt_of, cycle_rank, span_len, cache_slot)


def solution(mesh):
    placed = (P("inst", "tp"), P("inst", "tp"), P("tp", None), P(), P(), P(), P())
    return jax.shard_map(
        on_device,
        mesh=mesh,
        in_specs=placed,
        out_specs=(P("inst", "tp"), P("inst", None, "tp")),
        check_vma=False,
    )
```

```python
import functools
import math

import jax
import jax.numpy as jnp
from jax import lax
from jax.experimental import pallas as pl
from jax.experimental.pallas import tpu as pltpu
from jax.sharding import PartitionSpec as P

HD = 128
SPAN = 256
HEADS = 8
EARLIER = 6
KEYS = (EARLIER + 1) * SPAN
CHUNK = 512
ZROWS = 96
XROWS = SPAN - ZROWS
ZCUT, XCUT = 48, 80
PART = 128
NEG = -1e30
MESH = pl.DeviceIdType.MESH
COPIES = 96

PLAN = (
    "+zk1", "+zk3", "+zk2", "+zv3", "+zv1", "+v0d", "+k0d", "+k0u", "+v0u", "?v0d", "+fv0", "?k0u",
    "+fk0", "?zk1", "?zk3", "+k1u", "+zv2", "?k0d", "+xv0", "+k1d", "+k3u", "+k3d", "?zk2", "+k2d",
    "+k2u", "?v0u", "?k3d", "+fk3", "?k1u", "+xk1", "+fk1", "?zv3", "?fk0", "+v3u", "?k2d", "+fk2",
    "?k3u", "?k1d", "?k2u", "+xk0", "?fv0", "?zv1", "+xk12", "+v1u", "?xk0", "+v1d", "?xk12",
    "?fk3", "?zv2", "?fk1", "+xk8", "+xv1", "?xv0", "+v2u", "+v2d", "+xk4", "?fk2", "+xk10",
    "+v3d", "?v3u", "?xk8", "?xv1", "?xk1", "?v1u", "+fv3", "?xk4", "?xk10", "#", "#", "?v1d", "#",
    "+fv1", "?v2u", "+fv2", "#", "+xv12", "?v2d", "#", "#", "#", "#", "#", "#", "?v3d", "+xv4",
    "#", "#", "?fv3", "?xv12", "?fv1", "+xv8", "?fv2", "+xv10", "#", "#", "#", "#", "?xv4", "?xv8",
    "?xv10",
)

SUM_PLAN = (
    "!pvB", "!B21", "+r1b", "+r1a", "!pvA", "!A11", "!A21", "!A31", "+z12", "!B20", "+r0b", "+z11",
    "!B10", "+r0a", "!B11", "!A00", "!B31", "!B01", "!A20", "?r1b", "!eb1", "+x231", "?r1a",
    "!ea1", "+x211", "?z12", "!p2", "+t2a", "+z13", "?r0a", "!A30", "?r0b", "!B30", "!ea0", "+t2b",
    "!B00", "!A01", "+x210", "+z10", "!eb0", "+x230", "?x231", "?x211", "!q", "+z2", "?z13",
    "?z11", "?t2b", "!A10", "?t2a", "!p1", "+x11", "!p3", "+x13", "?z10", "!cache", "?z2", "?x210",
    "?x230", "!fl", "?x13", "?x11", "!fh",
)


def kernel(
    q_hbm, kv_hbm, w_hbm, prompt_hbm, rank_hbm, len_hbm, slot_hbm,
    mixed, cache,
    qbuf, kbuf, vbuf, wbuf, kcat, vcat, probs, totals, att,
    zsend, zrecv, own1, tsend, trecv, x1send, x1recv,
    rsend, rrecv, own2, x2send, x2recv, z2send, z2recv,
    prompt, rank, length, slot,
    local_sem, send_sem, recv_sem,
):
    me = lax.axis_index("inst")
    tp = lax.axis_index("tp")
    y, zh, core = me // 8, (me // 2) % 4, me % 2
    x, zl = tp // 2, tp % 2

    def inst_at(dy, dz, dc):
        return (((y + dy) % 4) * 4 + (zh + dz) % 4) * 2 + (core + dc) % 2

    def tp_at(dx, dz):
        return ((x + dx) % 4) * 2 + (zl + dz) % 2

    z_up, z_down = (inst_at(0, 1, 0), tp), (inst_at(0, 3, 0), tp)
    z_across = (inst_at(0, 2, 0), tp)
    y_up, y_down = (inst_at(1, 0, 0), tp), (inst_at(3, 0, 0), tp)
    sibling = (inst_at(0, 0, 1), tp)
    z_pair = (me, tp_at(0, 1))
    x_up, x_down = (me, tp_at(1, 0)), (me, tp_at(3, 0))

    n_local = [0]

    def local(src, dst):
        copy = pltpu.make_async_copy(src, dst, local_sem.at[n_local[0]])
        n_local[0] += 1
        copy.start()
        return copy

    own_k = local(kv_hbm.at[:, pl.ds(0, HD)], kbuf.at[0])
    own_v = local(kv_hbm.at[:, pl.ds(HD, HD)], vbuf.at[0])
    tables = [
        local(src, dst)
        for src, dst in (
            (prompt_hbm, prompt), (rank_hbm, rank), (len_hbm, length), (slot_hbm, slot)
        )
    ]
    q_copy = local(q_hbm, qbuf)

    barrier = pltpu.get_barrier_semaphore()
    friends = [z_up, z_down, z_across, y_up, y_down, sibling, z_pair, x_up, x_down]
    for friend in friends:
        pl.semaphore_signal(barrier, inc=1, device_id=friend, device_id_type=MESH)
    w_copies = {}
    for dz in (1, 0):
        for dx in (2, 1, 3, 0):
            columns = pl.ds(pl.multiple_of(tp_at(dx, dz) * CHUNK, CHUNK), CHUNK)
            w_copies[dx, dz] = local(w_hbm.at[:, columns], wbuf.at[dx * 2 + dz])
    pl.semaphore_wait(barrier, len(friends))

    sent = []

    def send(src, dst, device):
        index = len(sent)
        copy = pltpu.make_async_remote_copy(
            src_ref=src, dst_ref=dst, send_sem=send_sem.at[index], recv_sem=recv_sem.at[index],
            device_id=device, device_id_type=MESH,
        )
        copy.start()
        sent.append(copy)
        return copy

    bufs = {"k": kbuf, "v": vbuf}
    copies = {}

    def start_copy(name):
        if name[0] in "zfx":
            kind, buf, slot_at = name[0], bufs[name[1]], int(name[2:])
        else:
            kind, buf, slot_at = name[2], bufs[name[0]], int(name[1])
        onward_up = (slot_at < 2) == (buf is kbuf)
        source, target, count, device = {
            "z": lambda: {
                3: (0, 3, 1, z_up),
                1: (0, 1, 1, z_down),
                2: (0, 2, 1, z_across),
            }[slot_at],
            "u": lambda: (slot_at, 12 + slot_at, 1, y_up),
            "d": lambda: (slot_at, 4 + slot_at, 1, y_down),
            "f": lambda: (12 + slot_at, 8 + slot_at, 1, y_up)
            if onward_up
            else (4 + slot_at, 8 + slot_at, 1, y_down),
            "x": lambda: (
                slot_at, 16 + slot_at, {0: 1, 1: 3, 4: 4, 12: 4, 8: 2, 10: 2}[slot_at], sibling
            ),
        }[kind]()
        copies[name] = send(
            buf.at[pl.ds(source, count)], buf.at[pl.ds(target, count)], device
        )

    arrived = set()

    def arrive(name):
        if name not in arrived:
            arrived.add(name)
            copies[name].wait_recv()

    own_k.wait()
    own_v.wait()
    first_head = PLAN.index("#")
    for step in PLAN[:PLAN.index("?zk1")]:
        (start_copy if step[0] == "+" else arrive)(step[1:])

    for copy in tables:
        copy.wait()
    my_prompt, my_rank, my_len = prompt[me], rank[me], length[me]
    who, live = [me] * EARLIER, [jnp.int32(0)] * EARLIER
    for j in range(32):
        same, its_rank, its_len = prompt[j] == my_prompt, rank[j], length[j]
        for s in range(EARLIER):
            hit = same & (its_rank == s) & (s < my_rank)
            who[s] = jnp.where(hit, j, who[s])
            live[s] = jnp.where(hit, its_len, live[s])
    block_of = [jnp.int32(0)] * 2
    for b in range(64):
        for s in range(2):
            block_of[s] = jnp.where(slot[b] == 2 * me + s, b, block_of[s])

    def place(j):
        dy = ((j >> 3) + 4 - y) & 3
        dz = (((j >> 1) & 3) + 4 - zh) & 3
        dc = ((j & 1) + 2 - core) & 1
        return dc * 16 + dy * 4 + dz

    key_row = lax.broadcasted_iota(jnp.int32, (SPAN, HD), 0)
    first_lane = lax.broadcasted_iota(jnp.int32, (SPAN, HD), 1) == 0
    for s in range(EARLIER):
        dead = first_lane & (key_row >= live[s])
        kcat[s * SPAN:(s + 1) * SPAN, HD:] = jnp.where(dead, NEG, 0.0).astype(jnp.bfloat16)
    kcat[EARLIER * SPAN:, HD:] = jnp.zeros((SPAN, HD), jnp.bfloat16)

    for step in PLAN[PLAN.index("?zk1"):first_head]:
        (start_copy if step[0] == "+" else arrive)(step[1:])

    q_copy.wait()
    for s in range(EARLIER):
        kcat[s * SPAN:(s + 1) * SPAN, :HD] = kbuf[place(who[s])]
    kcat[EARLIER * SPAN:, :HD] = kbuf[0]
    factor = math.log2(math.e) / math.sqrt(HD)

    ones = (lax.broadcasted_iota(jnp.int32, (PART, HD), 1) == 0).astype(jnp.bfloat16)

    def weigh(head, start):
        rows = slice(start, start + PART)
        query = qbuf[rows, head * HD:(head + 1) * HD]
        scores = lax.dot_general(
            jnp.concatenate([query, ones], axis=1), kcat[...],
            (((1,), (1,)), ((), ())), preferred_element_type=jnp.float32,
        )
        earlier = scores[:, :EARLIER * SPAN]
        row = lax.broadcasted_iota(jnp.int32, (PART, SPAN), 0) + start
        column = lax.broadcasted_iota(jnp.int32, (PART, SPAN), 1)
        here = jnp.where(column <= row, scores[:, EARLIER * SPAN:], NEG)
        top = jnp.maximum(
            jnp.max(earlier, axis=1, keepdims=True), jnp.max(here, axis=1, keepdims=True)
        )
        earlier = jnp.exp2((earlier - top) * factor)
        here = jnp.exp2((here - top) * factor)
        total = jnp.sum(earlier, axis=1, keepdims=True) + jnp.sum(here, axis=1, keepdims=True)
        its_row = lax.broadcasted_iota(jnp.int32, (PART, 1), 0) + start
        inverse = jnp.where(its_row < my_len, 1.0 / total, 0.0)
        probs[head, rows, :EARLIER * SPAN] = earlier.astype(jnp.bfloat16)
        probs[head, rows, EARLIER * SPAN:] = here.astype(jnp.bfloat16)
        totals[head, rows, :] = jnp.broadcast_to(inverse, (PART, HD))

    weighed = 0
    for step in PLAN[first_head:]:
        if step == "#":
            weigh(weighed * PART // SPAN, weighed * PART % SPAN)
            weighed += 1
        else:
            (start_copy if step[0] == "+" else arrive)(step[1:])
    for name in copies:
        arrive(name)

    for s in range(EARLIER):
        vcat[s * SPAN:(s + 1) * SPAN, :] = vbuf[place(who[s])]
    vcat[EARLIER * SPAN:, :] = vbuf[0]

    def attend(rows):
        for head in range(HEADS):
            numer = jnp.dot(probs[head, rows, :], vcat[...], preferred_element_type=jnp.float32)
            attended = numer * totals[head, rows, :]
            att[rows, head * HD:(head + 1) * HD] = attended.astype(jnp.bfloat16)

    low, high = slice(0, ZROWS), slice(ZROWS, SPAN)
    ready = set()

    def project(rows, dx, dz):
        if (dx, dz) not in ready:
            ready.add((dx, dz))
            w_copies[dx, dz].wait()
        return jnp.dot(att[rows, :], wbuf[dx * 2 + dz], preferred_element_type=jnp.float32)

    def low_term(dx, dz):
        if dz:
            zsend[dx] = project(low, dx, dz).astype(jnp.bfloat16)
        else:
            own1[dx] = project(low, dx, dz)

    def high_term(dx, dz):
        if dx == 2:
            rsend[dz] = project(high, dx, dz).astype(jnp.bfloat16)
        else:
            own2[dz, {0: 0, 1: 1, 3: 2}[dx]] = project(high, dx, dz)

    def wide(values):
        return values.astype(jnp.float32)

    def pair_sum(dx):
        total = own1[dx] + wide(zrecv[dx])
        if dx == 2:
            tsend[...] = total.astype(jnp.bfloat16)
        elif dx == 1:
            x1send[0, :ZCUT, :] = (total[:ZCUT] + wide(trecv[:ZCUT, :])).astype(jnp.bfloat16)
            x1send[0, ZCUT:, :] = total[ZCUT:].astype(jnp.bfloat16)
        else:
            x1send[1, :ZCUT, :] = total[:ZCUT].astype(jnp.bfloat16)
            x1send[1, ZCUT:, :] = (total[ZCUT:] + wide(trecv[ZCUT:, :])).astype(jnp.bfloat16)

    def up_sum(dz):
        own = own2[dz, 1]
        x2send[dz, 0, :XCUT, :] = (own[:XCUT] + wide(rrecv[dz, :XCUT, :])).astype(jnp.bfloat16)
        x2send[dz, 0, XCUT:, :] = own[XCUT:].astype(jnp.bfloat16)

    def down_sum(dz):
        own = own2[dz, 2]
        x2send[dz, 1, :XCUT, :] = own[:XCUT].astype(jnp.bfloat16)
        x2send[dz, 1, XCUT:, :] = (own[XCUT:] + wide(rrecv[dz, XCUT:, :])).astype(jnp.bfloat16)

    def x_sum(dz):
        return own2[dz, 0] + wide(x2recv[dz, 0]) + wide(x2recv[dz, 1])

    def other_half():
        z2send[...] = x_sum(1).astype(jnp.bfloat16)

    def finish_high():
        mixed[high, :] = (x_sum(0) + wide(z2recv[...])).astype(jnp.bfloat16)

    def finish_low():
        total = own1[0] + wide(zrecv[0]) + wide(x1recv[0]) + wide(x1recv[1])
        mixed[low, :] = total.astype(jnp.bfloat16)

    def decode():
        for s in range(2):
            its, second = place(block_of[s] >> 1), (block_of[s] & 1) == 1
            for buf, at in ((kbuf, 0), (vbuf, HD)):
                block = buf[its]
                cache[s, :, at:at + HD] = jnp.where(second, block[SPAN // 2:], block[:SPAN // 2])

    steps = {
        "pvA": lambda: attend(low), "pvB": lambda: attend(high), "cache": decode,
        "q": other_half, "fl": finish_high, "fh": finish_low,
    }
    routes = {
        "z2": (z2send, z2recv, z_pair),
        "t2a": (tsend.at[pl.ds(0, ZCUT)], trecv.at[pl.ds(0, ZCUT)], x_up),
        "t2b": (
            tsend.at[pl.ds(ZCUT, ZROWS - ZCUT)], trecv.at[pl.ds(ZCUT, ZROWS - ZCUT)], x_down
        ),
        "x11": (x1send.at[0], x1recv.at[0], x_up),
        "x13": (x1send.at[1], x1recv.at[1], x_down),
    }
    for dx in range(4):
        routes[f"z1{dx}"] = (zsend.at[dx], zrecv.at[dx], z_pair)
        for dz in range(2):
            steps[f"A{dx}{dz}"] = functools.partial(low_term, dx, dz)
            steps[f"B{dx}{dz}"] = functools.partial(high_term, dx, dz)
    for dx in (1, 2, 3):
        steps[f"p{dx}"] = functools.partial(pair_sum, dx)
    for dz in range(2):
        steps[f"ea{dz}"] = functools.partial(up_sum, dz)
        steps[f"eb{dz}"] = functools.partial(down_sum, dz)
        for name, start, count, device in (
            (f"r{dz}a", 0, XCUT, x_up), (f"r{dz}b", XCUT, XROWS - XCUT, x_down)
        ):
            rows = pl.ds(start, count)
            routes[name] = (rsend.at[dz, rows], rrecv.at[dz, rows], device)
        routes[f"x21{dz}"] = (x2send.at[dz, 0], x2recv.at[dz, 0], x_up)
        routes[f"x23{dz}"] = (x2send.at[dz, 1], x2recv.at[dz, 1], x_down)
    for step in SUM_PLAN:
        name = step[1:]
        if step[0] == "+":
            copies[name] = send(*routes[name])
        elif step[0] == "?":
            arrive(name)
        else:
            steps[name]()

    for copy in sent:
        copy.wait_send()


def on_device(queries, key_values, out_weight, prompt_of, cycle_rank, span_len, cache_slot):
    bf16, f32 = jnp.bfloat16, jnp.float32
    width = HEADS * HD
    vmem = pltpu.VMEM
    return pl.pallas_call(
        kernel,
        out_shape=(
            vmem((SPAN, CHUNK), bf16),
            vmem((2, SPAN // 2, 2 * HD), bf16),
        ),
        in_specs=[pl.BlockSpec(memory_space=pl.ANY)] * 7,
        out_specs=(pl.BlockSpec(memory_space=pltpu.VMEM),) * 2,
        scratch_shapes=[
            vmem((SPAN, width), bf16),
            vmem((32, SPAN, HD), bf16),
            vmem((32, SPAN, HD), bf16),
            vmem((8, width, CHUNK), bf16),
            vmem((KEYS, 2 * HD), bf16),
            vmem((KEYS, HD), bf16),
            vmem((HEADS, SPAN, KEYS), bf16),
            vmem((HEADS, SPAN, HD), f32),
            vmem((SPAN, width), bf16),
            vmem((4, ZROWS, CHUNK), bf16),
            vmem((4, ZROWS, CHUNK), bf16),
            vmem((4, ZROWS, CHUNK), f32),
            vmem((ZROWS, CHUNK), bf16),
            vmem((ZROWS, CHUNK), bf16),
            vmem((2, ZROWS, CHUNK), bf16),
            vmem((2, ZROWS, CHUNK), bf16),
            vmem((2, XROWS, CHUNK), bf16),
            vmem((2, XROWS, CHUNK), bf16),
            vmem((2, 3, XROWS, CHUNK), f32),
            vmem((2, 2, XROWS, CHUNK), bf16),
            vmem((2, 2, XROWS, CHUNK), bf16),
            vmem((XROWS, CHUNK), bf16),
            vmem((XROWS, CHUNK), bf16),
            pltpu.SMEM((32,), jnp.int32),
            pltpu.SMEM((32,), jnp.int32),
            pltpu.SMEM((32,), jnp.int32),
            pltpu.SMEM((64,), jnp.int32),
            pltpu.SemaphoreType.DMA((24,)),
            pltpu.SemaphoreType.DMA((COPIES,)),
            pltpu.SemaphoreType.DMA((COPIES,)),
        ],
        compiler_params=pltpu.CompilerParams(
            collective_id=0, has_side_effects=True, vmem_limit_bytes=56 * 1024 * 1024
        ),
        cost_estimate=pl.CostEstimate(
            flops=4 * SPAN * HEADS * KEYS * HD + 2 * SPAN * width * 4096,
            bytes_accessed=10 * 1024 * 1024,
            transcendentals=HEADS * SPAN * KEYS,
        ),
    )(queries, key_values, out_weight, prompt_of, cycle_rank, span_len, cache_slot)


def solution(mesh):
    placed = (P("inst", "tp"), P("inst", "tp"), P("tp", None), P(), P(), P(), P())
    return jax.shard_map(
        on_device,
        mesh=mesh,
        in_specs=placed,
        out_specs=(P("inst", "tp"), P("inst", None, "tp")),
        check_vma=False,
    )
```

```python
import functools
import math

import jax
import jax.numpy as jnp
from jax import lax
from jax.experimental import pallas as pl
from jax.experimental.pallas import tpu as pltpu
from jax.sharding import PartitionSpec as P

HD = 128
SPAN = 256
HEADS = 8
EARLIER = 6
KEYS = (EARLIER + 1) * SPAN
CHUNK = 512
ZROWS = 112
XROWS = SPAN - ZROWS
ZCUT, XCUT = 48, 64
PART = SPAN
NEG = -1e30
MESH = pl.DeviceIdType.MESH
COPIES = 128
PIECES = ((0, 0, 128), (0, 128, 128), (1, 0, 128), (1, 128, 128))
SIBLING_FAR = 4

PLAN = (
    10301, 14300, 14000, 10003, 10203, 14200, 15100, 15300, 19100, 10101, 10103, 10001, 15000,
    15200, 0, 14100, 25100, 24000, 17100, 24300, 16000, 20301, 12302, 14301, 20003, 15003, 11002,
    16300, 14003, 15301, 20101, 15101, 12102, 20203, 11202, 14101, 14203, 15203, 20001, 15001,
    19000, 27100, 14001, 20103, 25003, 10303, 14103, 15103, 10201, 17003, 24301, 22302, 14302,
    19300, 21002, 15002, 19001, 25101, 14002, 17101, 22102, 14102, 15302, 24001, 25000, 26300,
    21202, 25200, 25301, 14202, 24200, 15102, 15202, 16001, 24003, 24203, 25002, 20303, 15303,
    24103, 17002, 16103, 25001, 19200, 26000, 20201, 14303, 24102, 16102, 19301, 19101, 16301,
    24002, 29100, 14201, 24101, 15201, 25102, 19004, 19201, 25302, 24302, 17200, 25103, 26001,
    29000, 27101, 27003, 25202, 17302, 25300, 19104, 26103, 19012, 24100, 16203, 25303, 29101,
    17303, 24202, 19304, 27002, 19112, 16202, 19008, 25203, 24303, 26102, 19108, 29301, 25201,
    17201, 26301, 29200, 27302, 29304, 29104, 19204, 29012, 24201, 29112, 29300, 29201, 19312,
    29004, 27200, 29008, 19212, 29001, 26203, 27303, 19308, 29108, 1, 1, 26202, 1, 27201, 19208, 1,
    1, 1, 1, 29312, 29212, 29204, 29308, 1, 29208,
)

SUM_PLAN = (
    "!pvB", "!B21", "+r1b", "+r1a", "!pvA", "!A21", "+z12", "!B20", "+r0b", "!B10", "!B30", "!B31",
    "+r0a", "!A01", "!B11", "!A11", "+z11", "!A31", "?r1a", "!ea1", "+x211", "+z13", "?r1b",
    "!eb1", "+x231", "!A20", "?z12", "!p2", "!B01", "?r0b", "+t2a", "!eb0", "?r0a", "!A10", "!A30",
    "+t2b", "!ea0", "+x230", "+x210", "+z10", "!B00", "?x231", "?x211", "!q", "?t2a", "!A00",
    "+z2", "?z11", "?t2b", "!p1", "?z13", "+x11", "!p3", "+x13", "?x210", "!cache", "?x11", "?z10",
    "?x230", "?z2", "!fl", "?x13", "!fh",
)


def kernel(
    q_hbm, kv_hbm, w_hbm, prompt_hbm, rank_hbm, len_hbm, slot_hbm,
    mixed, cache,
    qbuf, kbuf, vbuf, wbuf, kcat, vcat, probs, totals, att,
    zsend, zrecv, own1, tsend, trecv, x1send, x1recv,
    rsend, rrecv, own2, x2send, x2recv, z2send, z2recv,
    prompt, rank, length, slot,
    local_sem, send_sem, recv_sem,
):
    me = lax.axis_index("inst")
    tp = lax.axis_index("tp")
    y, zh, core = me // 8, (me // 2) % 4, me % 2
    x, zl = tp // 2, tp % 2

    def inst_at(dy, dz, dc):
        return (((y + dy) % 4) * 4 + (zh + dz) % 4) * 2 + (core + dc) % 2

    def tp_at(dx, dz):
        return ((x + dx) % 4) * 2 + (zl + dz) % 2

    z_up, z_down = (inst_at(0, 1, 0), tp), (inst_at(0, 3, 0), tp)
    z_across, y_across = (inst_at(0, 2, 0), tp), (inst_at(2, 0, 0), tp)
    y_up, y_down = (inst_at(1, 0, 0), tp), (inst_at(3, 0, 0), tp)
    sibling = (inst_at(0, 0, 1), tp)
    z_pair = (me, tp_at(0, 1))
    x_up, x_down = (me, tp_at(1, 0)), (me, tp_at(3, 0))

    n_local = [0]

    def local(src, dst):
        copy = pltpu.make_async_copy(src, dst, local_sem.at[n_local[0]])
        n_local[0] += 1
        copy.start()
        return copy

    own_k = local(kv_hbm.at[:, pl.ds(0, HD)], kbuf.at[0])
    own_v = local(kv_hbm.at[:, pl.ds(HD, HD)], vbuf.at[0])
    tables = [
        local(src, dst)
        for src, dst in (
            (prompt_hbm, prompt), (rank_hbm, rank), (len_hbm, length), (slot_hbm, slot)
        )
    ]
    q_copy = local(q_hbm, qbuf)

    barrier = pltpu.get_barrier_semaphore()
    friends = [z_up, z_down, y_up, y_down, sibling, z_pair, x_up, x_down]
    for friend in friends:
        pl.semaphore_signal(barrier, inc=1, device_id=friend, device_id_type=MESH)
    w_copies = {}
    for dz in (1, 0):
        for dx in (2, 1, 3, 0):
            columns = pl.ds(pl.multiple_of(tp_at(dx, dz) * CHUNK, CHUNK), CHUNK)
            w_copies[dx, dz] = local(w_hbm.at[:, columns], wbuf.at[dx * 2 + dz])
    pl.semaphore_wait(barrier, len(friends))

    sent = []

    def send(src, dst, device):
        index = len(sent)
        copy = pltpu.make_async_remote_copy(
            src_ref=src, dst_ref=dst, send_sem=send_sem.at[index], recv_sem=recv_sem.at[index],
            device_id=device, device_id_type=MESH,
        )
        copy.start()
        sent.append(copy)
        return copy

    copies = {}

    def start_copy(code):
        kind, piece, at = code // 1000, code // 100 % 10, code % 100
        which, first_row, rows = PIECES[piece]
        source, target, device = (
            (0, at, z_up if at == 3 else z_down),
            (3, at, z_up), (1, at, z_down), (0, at, z_across),
            (at, 12 + at, y_up), (at, 4 + at, y_down),
            (12 + at, 8 + at, y_up), (4 + at, 8 + at, y_down), (at, 8 + at, y_across),
            (at, 16 + at, sibling),
        )[kind]
        count = {0: 1, 1: 3, 4: 4, 12: 4, 8: SIBLING_FAR, 10: 2}[at] if kind == 9 else 1
        buf, piece_rows = (kbuf, vbuf)[which], pl.ds(first_row, rows)
        copies[code] = send(
            buf.at[pl.ds(source, count), piece_rows], buf.at[pl.ds(target, count), piece_rows], device
        )

    arrived = set()

    def arrive(name):
        if name not in arrived:
            arrived.add(name)
            copies[name].wait_recv()

    own_k.wait()
    own_v.wait()
    needs = {}

    def look_up():
        for copy in tables:
            copy.wait()
        my_prompt, my_rank, my_len = prompt[me], rank[me], length[me]
        who, live = [me] * EARLIER, [jnp.int32(0)] * EARLIER
        for j in range(32):
            same, its_rank, its_len = prompt[j] == my_prompt, rank[j], length[j]
            for s in range(EARLIER):
                hit = same & (its_rank == s) & (s < my_rank)
                who[s] = jnp.where(hit, j, who[s])
                live[s] = jnp.where(hit, its_len, live[s])
        block_of = [jnp.int32(0)] * 2
        for b in range(64):
            for s in range(2):
                block_of[s] = jnp.where(slot[b] == 2 * me + s, b, block_of[s])
        needs.update(who=who, block_of=block_of, my_len=my_len)
        key_row = lax.broadcasted_iota(jnp.int32, (SPAN, HD), 0)
        first_lane = lax.broadcasted_iota(jnp.int32, (SPAN, HD), 1) == 0
        for s in range(EARLIER):
            dead = first_lane & (key_row >= live[s])
            kcat[s * SPAN:(s + 1) * SPAN, HD:] = jnp.where(dead, NEG, 0.0).astype(jnp.bfloat16)
        kcat[EARLIER * SPAN:, HD:] = jnp.zeros((SPAN, HD), jnp.bfloat16)

    def place(j):
        dy = ((j >> 3) + 4 - y) & 3
        dz = (((j >> 1) & 3) + 4 - zh) & 3
        dc = ((j & 1) + 2 - core) & 1
        return dc * 16 + dy * 4 + dz

    def take_keys():
        q_copy.wait()
        for s in range(EARLIER):
            kcat[s * SPAN:(s + 1) * SPAN, :HD] = kbuf[place(needs["who"][s])]
        kcat[EARLIER * SPAN:, :HD] = kbuf[0]

    factor = math.log2(math.e) / math.sqrt(HD)

    ones = (lax.broadcasted_iota(jnp.int32, (PART, HD), 1) == 0).astype(jnp.bfloat16)

    def weigh(head, start):
        rows = slice(start, start + PART)
        query = qbuf[rows, head * HD:(head + 1) * HD]
        scores = lax.dot_general(
            jnp.concatenate([query, ones], axis=1), kcat[...],
            (((1,), (1,)), ((), ())), preferred_element_type=jnp.float32,
        )
        earlier = scores[:, :EARLIER * SPAN]
        row = lax.broadcasted_iota(jnp.int32, (PART, SPAN), 0) + start
        column = lax.broadcasted_iota(jnp.int32, (PART, SPAN), 1)
        here = jnp.where(column <= row, scores[:, EARLIER * SPAN:], NEG)
        top = jnp.maximum(
            jnp.max(earlier, axis=1, keepdims=True), jnp.max(here, axis=1, keepdims=True)
        )
        earlier = jnp.exp2((earlier - top) * factor)
        here = jnp.exp2((here - top) * factor)
        total = jnp.sum(earlier, axis=1, keepdims=True) + jnp.sum(here, axis=1, keepdims=True)
        its_row = lax.broadcasted_iota(jnp.int32, (PART, 1), 0) + start
        inverse = jnp.where(its_row < needs["my_len"], 1.0 / total, 0.0)
        probs[head, rows, :EARLIER * SPAN] = earlier.astype(jnp.bfloat16)
        probs[head, rows, EARLIER * SPAN:] = here.astype(jnp.bfloat16)
        totals[head, rows, :] = jnp.broadcast_to(inverse, (PART, HD))

    weighed = 0
    for step in PLAN:
        if step == 0:
            look_up()
        elif step == 1:
            if not weighed:
                take_keys()
            weigh(weighed, 0)
            weighed += 1
        elif step < 20000:
            start_copy(step - 10000)
        else:
            arrive(step - 20000)
    for name in copies:
        arrive(name)

    for s in range(EARLIER):
        vcat[s * SPAN:(s + 1) * SPAN, :] = vbuf[place(needs["who"][s])]
    vcat[EARLIER * SPAN:, :] = vbuf[0]

    def attend(rows):
        for head in range(HEADS):
            numer = jnp.dot(probs[head, rows, :], vcat[...], preferred_element_type=jnp.float32)
            attended = numer * totals[head, rows, :]
            att[rows, head * HD:(head + 1) * HD] = attended.astype(jnp.bfloat16)

    low, high = slice(0, ZROWS), slice(ZROWS, SPAN)
    ready = set()

    def project(rows, dx, dz):
        if (dx, dz) not in ready:
            ready.add((dx, dz))
            w_copies[dx, dz].wait()
        return jnp.dot(att[rows, :], wbuf[dx * 2 + dz], preferred_element_type=jnp.float32)

    def low_term(dx, dz):
        if dz:
            zsend[dx] = project(low, dx, dz).astype(jnp.bfloat16)
        else:
            own1[dx] = project(low, dx, dz)

    def high_term(dx, dz):
        if dx == 2:
            rsend[dz] = project(high, dx, dz).astype(jnp.bfloat16)
        else:
            own2[dz, {0: 0, 1: 1, 3: 2}[dx]] = project(high, dx, dz)

    def wide(values):
        return values.astype(jnp.float32)

    def pair_sum(dx):
        total = own1[dx] + wide(zrecv[dx])
        if dx == 2:
            tsend[...] = total.astype(jnp.bfloat16)
        elif dx == 1:
            x1send[0, :ZCUT, :] = (total[:ZCUT] + wide(trecv[:ZCUT, :])).astype(jnp.bfloat16)
            x1send[0, ZCUT:, :] = total[ZCUT:].astype(jnp.bfloat16)
        else:
            x1send[1, :ZCUT, :] = total[:ZCUT].astype(jnp.bfloat16)
            x1send[1, ZCUT:, :] = (total[ZCUT:] + wide(trecv[ZCUT:, :])).astype(jnp.bfloat16)

    def up_sum(dz):
        own = own2[dz, 1]
        x2send[dz, 0, :XCUT, :] = (own[:XCUT] + wide(rrecv[dz, :XCUT, :])).astype(jnp.bfloat16)
        x2send[dz, 0, XCUT:, :] = own[XCUT:].astype(jnp.bfloat16)

    def down_sum(dz):
        own = own2[dz, 2]
        x2send[dz, 1, :XCUT, :] = own[:XCUT].astype(jnp.bfloat16)
        x2send[dz, 1, XCUT:, :] = (own[XCUT:] + wide(rrecv[dz, XCUT:, :])).astype(jnp.bfloat16)

    def x_sum(dz):
        return own2[dz, 0] + wide(x2recv[dz, 0]) + wide(x2recv[dz, 1])

    def other_half():
        z2send[...] = x_sum(1).astype(jnp.bfloat16)

    def finish_high():
        mixed[high, :] = (x_sum(0) + wide(z2recv[...])).astype(jnp.bfloat16)

    def finish_low():
        total = own1[0] + wide(zrecv[0]) + wide(x1recv[0]) + wide(x1recv[1])
        mixed[low, :] = total.astype(jnp.bfloat16)

    def decode():
        for s in range(2):
            its, second = place(needs["block_of"][s] >> 1), (needs["block_of"][s] & 1) == 1
            for buf, at in ((kbuf, 0), (vbuf, HD)):
                block = buf[its]
                cache[s, :, at:at + HD] = jnp.where(second, block[SPAN // 2:], block[:SPAN // 2])

    steps = {
        "pvA": lambda: attend(low), "pvB": lambda: attend(high), "cache": decode,
        "q": other_half, "fl": finish_high, "fh": finish_low,
    }
    routes = {
        "z2": (z2send, z2recv, z_pair),
        "t2a": (tsend.at[pl.ds(0, ZCUT)], trecv.at[pl.ds(0, ZCUT)], x_up),
        "t2b": (
            tsend.at[pl.ds(ZCUT, ZROWS - ZCUT)], trecv.at[pl.ds(ZCUT, ZROWS - ZCUT)], x_down
        ),
        "x11": (x1send.at[0], x1recv.at[0], x_up),
        "x13": (x1send.at[1], x1recv.at[1], x_down),
    }
    for dx in range(4):
        routes[f"z1{dx}"] = (zsend.at[dx], zrecv.at[dx], z_pair)
        for dz in range(2):
            steps[f"A{dx}{dz}"] = functools.partial(low_term, dx, dz)
            steps[f"B{dx}{dz}"] = functools.partial(high_term, dx, dz)
    for dx in (1, 2, 3):
        steps[f"p{dx}"] = functools.partial(pair_sum, dx)
    for dz in range(2):
        steps[f"ea{dz}"] = functools.partial(up_sum, dz)
        steps[f"eb{dz}"] = functools.partial(down_sum, dz)
        for name, start, count, device in (
            (f"r{dz}a", 0, XCUT, x_up), (f"r{dz}b", XCUT, XROWS - XCUT, x_down)
        ):
            rows = pl.ds(start, count)
            routes[name] = (rsend.at[dz, rows], rrecv.at[dz, rows], device)
        routes[f"x21{dz}"] = (x2send.at[dz, 0], x2recv.at[dz, 0], x_up)
        routes[f"x23{dz}"] = (x2send.at[dz, 1], x2recv.at[dz, 1], x_down)
    for step in SUM_PLAN:
        name = step[1:]
        if step[0] == "+":
            copies[name] = send(*routes[name])
        elif step[0] == "?":
            arrive(name)
        else:
            steps[name]()

    for copy in sent:
        copy.wait_send()


def on_device(queries, key_values, out_weight, prompt_of, cycle_rank, span_len, cache_slot):
    bf16, f32 = jnp.bfloat16, jnp.float32
    width = HEADS * HD
    vmem = pltpu.VMEM
    return pl.pallas_call(
        kernel,
        out_shape=(
            vmem((SPAN, CHUNK), bf16),
            vmem((2, SPAN // 2, 2 * HD), bf16),
        ),
        in_specs=[pl.BlockSpec(memory_space=pl.ANY)] * 7,
        out_specs=(pl.BlockSpec(memory_space=pltpu.VMEM),) * 2,
        scratch_shapes=[
            vmem((SPAN, width), bf16),
            vmem((32, SPAN, HD), bf16),
            vmem((32, SPAN, HD), bf16),
            vmem((8, width, CHUNK), bf16),
            vmem((KEYS, 2 * HD), bf16),
            vmem((KEYS, HD), bf16),
            vmem((HEADS, SPAN, KEYS), bf16),
            vmem((HEADS, SPAN, HD), f32),
            vmem((SPAN, width), bf16),
            vmem((4, ZROWS, CHUNK), bf16),
            vmem((4, ZROWS, CHUNK), bf16),
            vmem((4, ZROWS, CHUNK), f32),
            vmem((ZROWS, CHUNK), bf16),
            vmem((ZROWS, CHUNK), bf16),
            vmem((2, ZROWS, CHUNK), bf16),
            vmem((2, ZROWS, CHUNK), bf16),
            vmem((2, XROWS, CHUNK), bf16),
            vmem((2, XROWS, CHUNK), bf16),
            vmem((2, 3, XROWS, CHUNK), f32),
            vmem((2, 2, XROWS, CHUNK), bf16),
            vmem((2, 2, XROWS, CHUNK), bf16),
            vmem((XROWS, CHUNK), bf16),
            vmem((XROWS, CHUNK), bf16),
            pltpu.SMEM((32,), jnp.int32),
            pltpu.SMEM((32,), jnp.int32),
            pltpu.SMEM((32,), jnp.int32),
            pltpu.SMEM((64,), jnp.int32),
            pltpu.SemaphoreType.DMA((24,)),
            pltpu.SemaphoreType.DMA((COPIES,)),
            pltpu.SemaphoreType.DMA((COPIES,)),
        ],
        compiler_params=pltpu.CompilerParams(
            collective_id=0, has_side_effects=True, vmem_limit_bytes=56 * 1024 * 1024
        ),
        cost_estimate=pl.CostEstimate(
            flops=4 * SPAN * HEADS * KEYS * HD + 2 * SPAN * width * 4096,
            bytes_accessed=10 * 1024 * 1024,
            transcendentals=HEADS * SPAN * KEYS,
        ),
    )(queries, key_values, out_weight, prompt_of, cycle_rank, span_len, cache_slot)


def solution(mesh):
    placed = (P("inst", "tp"), P("inst", "tp"), P("tp", None), P(), P(), P(), P())
    return jax.shard_map(
        on_device,
        mesh=mesh,
        in_specs=placed,
        out_specs=(P("inst", "tp"), P("inst", None, "tp")),
        check_vma=False,
    )
```

```python
import functools
import math

import jax
import jax.numpy as jnp
from jax import lax
from jax.experimental import pallas as pl
from jax.experimental.pallas import tpu as pltpu
from jax.sharding import PartitionSpec as P

HD = 128
SPAN = 256
HEADS = 8
EARLIER = 6
KEYS = (EARLIER + 1) * SPAN
CHUNK = 512
ZROWS = 112
XROWS = SPAN - ZROWS
ZCUT, XCUT = 48, 64
PART = SPAN
NEG = -1e30
MESH = pl.DeviceIdType.MESH
COPIES = 128
PIECES = ((0, 0, 128), (0, 128, 128), (1, 0, 128), (1, 128, 128))
SIBLING_FAR = 4

PLAN = (
    10003, 10101, 14200, 19100, 15100, 14300, 14000, 10001, 10203, 10103, 15200, 14100, 15300,
    15000, 10301, 25100, 17100, 19300, 25200, 17200, 24300, 16300, 20003, 11002, 20101, 14003,
    12102, 15003, 10303, 15101, 14101, 10201, 20203, 15203, 14203, 19000, 20001, 15001, 14001,
    24000, 16000, 20103, 11202, 15103, 25003, 20301, 15301, 12302, 14103, 14301, 17003, 24003,
    25101, 22102, 14102, 21002, 15002, 14002, 24001, 15102, 25001, 20303, 16001, 24100, 27200,
    19200, 25000, 15303, 24103, 17101, 29100, 16103, 20201, 21202, 14202, 19001, 15201, 24102,
    25002, 25203, 24301, 16102, 24101, 19112, 14201, 17002, 22302, 27100, 15302, 14302, 19004,
    14303, 0, 26300, 15202, 25303, 25102, 25103, 29001, 26001, 19101, 24002, 25301, 26103, 29300,
    29000, 19012, 19104, 19201, 24200, 17303, 29200, 24203, 27003, 29004, 19301, 24202, 25300,
    16202, 16203, 27101, 29112, 26000, 25201, 17201, 26102, 19108, 16301, 27002, 19008, 25302,
    17302, 25202, 29104, 19204, 19304, 24201, 24303, 24302, 29108, 29012, 29101, 29201, 19212,
    19312, 29301, 29008, 1, 1, 27303, 26203, 27201, 26202, 19208, 1, 27302, 29204, 26301, 19308,
    29304, 1, 29212, 1, 29312, 1, 1, 1, 29208, 29308,
)

SUM_PLAN = (
    "!pvB", "!B21", "+r1b", "+r1a", "!pvA", "!A21", "+z12", "!B20", "+r0b", "!B10", "!B30", "!B31",
    "+r0a", "!A01", "!B11", "!A11", "+z11", "!A31", "?r1a", "!ea1", "+x211", "+z13", "?r1b",
    "!eb1", "+x231", "!A20", "?z12", "!p2", "!B01", "?r0b", "+t2a", "!eb0", "?r0a", "!A10", "!A30",
    "+t2b", "!ea0", "+x230", "+x210", "+z10", "!B00", "?x231", "?x211", "!q", "?t2a", "!A00",
    "+z2", "?z11", "?t2b", "!p1", "?z13", "+x11", "!p3", "+x13", "?x210", "!cache", "?x11", "?z10",
    "?x230", "?z2", "!fl", "?x13", "!fh",
)


def kernel(
    q_hbm, kv_hbm, w_hbm, prompt_hbm, rank_hbm, len_hbm, slot_hbm,
    mixed, cache,
    qbuf, kbuf, vbuf, wbuf, kcat, vcat, probs, totals, att,
    zsend, zrecv, own1, tsend, trecv, x1send, x1recv,
    rsend, rrecv, own2, x2send, x2recv, z2send, z2recv,
    prompt, rank, length, slot,
    local_sem, send_sem, recv_sem,
):
    me = lax.axis_index("inst")
    tp = lax.axis_index("tp")
    y, zh, core = me // 8, (me // 2) % 4, me % 2
    x, zl = tp // 2, tp % 2

    def inst_at(dy, dz, dc):
        return (((y + dy) % 4) * 4 + (zh + dz) % 4) * 2 + (core + dc) % 2

    def tp_at(dx, dz):
        return ((x + dx) % 4) * 2 + (zl + dz) % 2

    z_up, z_down = (inst_at(0, 1, 0), tp), (inst_at(0, 3, 0), tp)
    z_across, y_across = (inst_at(0, 2, 0), tp), (inst_at(2, 0, 0), tp)
    y_up, y_down = (inst_at(1, 0, 0), tp), (inst_at(3, 0, 0), tp)
    sibling = (inst_at(0, 0, 1), tp)
    z_pair = (me, tp_at(0, 1))
    x_up, x_down = (me, tp_at(1, 0)), (me, tp_at(3, 0))

    n_local = [0]

    def local(src, dst):
        copy = pltpu.make_async_copy(src, dst, local_sem.at[n_local[0]])
        n_local[0] += 1
        copy.start()
        return copy

    own_k = local(kv_hbm.at[:, pl.ds(0, HD)], kbuf.at[0])
    own_v = local(kv_hbm.at[:, pl.ds(HD, HD)], vbuf.at[0])
    tables = [
        local(src, dst)
        for src, dst in (
            (prompt_hbm, prompt), (rank_hbm, rank), (len_hbm, length), (slot_hbm, slot)
        )
    ]
    q_copy = local(q_hbm, qbuf)

    barrier = pltpu.get_barrier_semaphore()
    friends = [z_up, z_down, y_up, y_down, sibling, z_pair, x_up, x_down]
    for friend in friends:
        pl.semaphore_signal(barrier, inc=1, device_id=friend, device_id_type=MESH)
    w_copies = {}
    for dz in (1, 0):
        for dx in (2, 1, 3, 0):
            columns = pl.ds(pl.multiple_of(tp_at(dx, dz) * CHUNK, CHUNK), CHUNK)
            w_copies[dx, dz] = local(w_hbm.at[:, columns], wbuf.at[dx * 2 + dz])
    pl.semaphore_wait(barrier, len(friends))

    sent = []

    def send(src, dst, device):
        index = len(sent)
        copy = pltpu.make_async_remote_copy(
            src_ref=src, dst_ref=dst, send_sem=send_sem.at[index], recv_sem=recv_sem.at[index],
            device_id=device, device_id_type=MESH,
        )
        copy.start()
        sent.append(copy)
        return copy

    copies = {}

    def start_copy(code):
        kind, piece, at = code // 1000, code // 100 % 10, code % 100
        which, first_row, rows = PIECES[piece]
        source, target, device = (
            (0, at, z_up if at == 3 else z_down),
            (3, at, z_up), (1, at, z_down), (0, at, z_across),
            (at, 12 + at, y_up), (at, 4 + at, y_down),
            (12 + at, 8 + at, y_up), (4 + at, 8 + at, y_down), (at, 8 + at, y_across),
            (at, 16 + at, sibling),
        )[kind]
        count = {0: 1, 1: 3, 4: 4, 12: 4, 8: SIBLING_FAR, 10: 2}[at] if kind == 9 else 1
        buf, piece_rows = (kbuf, vbuf)[which], pl.ds(first_row, rows)
        copies[code] = send(
            buf.at[pl.ds(source, count), piece_rows], buf.at[pl.ds(target, count), piece_rows], device
        )

    arrived = set()

    def arrive(name):
        if name not in arrived:
            arrived.add(name)
            copies[name].wait_recv()

    own_k.wait()
    own_v.wait()
    needs = {}

    def look_up():
        for copy in tables:
            copy.wait()
        my_prompt, my_rank, my_len = prompt[me], rank[me], length[me]
        who, live = [me] * EARLIER, [jnp.int32(0)] * EARLIER
        for j in range(32):
            same, its_rank, its_len = prompt[j] == my_prompt, rank[j], length[j]
            for s in range(EARLIER):
                hit = same & (its_rank == s) & (s < my_rank)
                who[s] = jnp.where(hit, j, who[s])
                live[s] = jnp.where(hit, its_len, live[s])
        block_of = [jnp.int32(0)] * 2
        for b in range(64):
            for s in range(2):
                block_of[s] = jnp.where(slot[b] == 2 * me + s, b, block_of[s])
        needs.update(who=who, block_of=block_of, my_len=my_len)
        key_row = lax.broadcasted_iota(jnp.int32, (SPAN, HD), 0)
        first_lane = lax.broadcasted_iota(jnp.int32, (SPAN, HD), 1) == 0
        for s in range(EARLIER):
            dead = first_lane & (key_row >= live[s])
            kcat[s * SPAN:(s + 1) * SPAN, HD:] = jnp.where(dead, NEG, 0.0).astype(jnp.bfloat16)
        kcat[EARLIER * SPAN:, HD:] = jnp.zeros((SPAN, HD), jnp.bfloat16)

    def place(j):
        dy = ((j >> 3) + 4 - y) & 3
        dz = (((j >> 1) & 3) + 4 - zh) & 3
        dc = ((j & 1) + 2 - core) & 1
        return dc * 16 + dy * 4 + dz

    def take_keys():
        q_copy.wait()
        for s in range(EARLIER):
            kcat[s * SPAN:(s + 1) * SPAN, :HD] = kbuf[place(needs["who"][s])]
        kcat[EARLIER * SPAN:, :HD] = kbuf[0]

    factor = math.log2(math.e) / math.sqrt(HD)

    ones = (lax.broadcasted_iota(jnp.int32, (PART, HD), 1) == 0).astype(jnp.bfloat16)

    def weigh(head, start):
        rows = slice(start, start + PART)
        query = qbuf[rows, head * HD:(head + 1) * HD]
        scores = lax.dot_general(
            jnp.concatenate([query, ones], axis=1), kcat[...],
            (((1,), (1,)), ((), ())), preferred_element_type=jnp.float32,
        )
        earlier = scores[:, :EARLIER * SPAN]
        row = lax.broadcasted_iota(jnp.int32, (PART, SPAN), 0) + start
        column = lax.broadcasted_iota(jnp.int32, (PART, SPAN), 1)
        here = jnp.where(column <= row, scores[:, EARLIER * SPAN:], NEG)
        top = jnp.maximum(
            jnp.max(earlier, axis=1, keepdims=True), jnp.max(here, axis=1, keepdims=True)
        )
        earlier = jnp.exp2((earlier - top) * factor)
        here = jnp.exp2((here - top) * factor)
        total = jnp.sum(earlier, axis=1, keepdims=True) + jnp.sum(here, axis=1, keepdims=True)
        its_row = lax.broadcasted_iota(jnp.int32, (PART, 1), 0) + start
        inverse = jnp.where(its_row < needs["my_len"], 1.0 / total, 0.0)
        probs[head, rows, :EARLIER * SPAN] = earlier.astype(jnp.bfloat16)
        probs[head, rows, EARLIER * SPAN:] = here.astype(jnp.bfloat16)
        totals[head, rows, :] = jnp.broadcast_to(inverse, (PART, HD))

    weighed = 0
    for step in PLAN:
        if step == 0:
            look_up()
        elif step == 1:
            if not weighed:
                take_keys()
            weigh(weighed, 0)
            weighed += 1
        elif step < 20000:
            start_copy(step - 10000)
        else:
            arrive(step - 20000)
    for name in copies:
        arrive(name)

    for s in range(EARLIER):
        vcat[s * SPAN:(s + 1) * SPAN, :] = vbuf[place(needs["who"][s])]
    vcat[EARLIER * SPAN:, :] = vbuf[0]

    def attend(rows):
        for head in range(HEADS):
            numer = jnp.dot(probs[head, rows, :], vcat[...], preferred_element_type=jnp.float32)
            attended = numer * totals[head, rows, :]
            att[rows, head * HD:(head + 1) * HD] = attended.astype(jnp.bfloat16)

    low, high = slice(0, ZROWS), slice(ZROWS, SPAN)
    ready = set()

    def project(rows, dx, dz):
        if (dx, dz) not in ready:
            ready.add((dx, dz))
            w_copies[dx, dz].wait()
        return jnp.dot(att[rows, :], wbuf[dx * 2 + dz], preferred_element_type=jnp.float32)

    def low_term(dx, dz):
        if dz:
            zsend[dx] = project(low, dx, dz).astype(jnp.bfloat16)
        else:
            own1[dx] = project(low, dx, dz)

    def high_term(dx, dz):
        if dx == 2:
            rsend[dz] = project(high, dx, dz).astype(jnp.bfloat16)
        else:
            own2[dz, {0: 0, 1: 1, 3: 2}[dx]] = project(high, dx, dz)

    def wide(values):
        return values.astype(jnp.float32)

    def pair_sum(dx):
        total = own1[dx] + wide(zrecv[dx])
        if dx == 2:
            tsend[...] = total.astype(jnp.bfloat16)
        elif dx == 1:
            x1send[0, :ZCUT, :] = (total[:ZCUT] + wide(trecv[:ZCUT, :])).astype(jnp.bfloat16)
            x1send[0, ZCUT:, :] = total[ZCUT:].astype(jnp.bfloat16)
        else:
            x1send[1, :ZCUT, :] = total[:ZCUT].astype(jnp.bfloat16)
            x1send[1, ZCUT:, :] = (total[ZCUT:] + wide(trecv[ZCUT:, :])).astype(jnp.bfloat16)

    def up_sum(dz):
        own = own2[dz, 1]
        x2send[dz, 0, :XCUT, :] = (own[:XCUT] + wide(rrecv[dz, :XCUT, :])).astype(jnp.bfloat16)
        x2send[dz, 0, XCUT:, :] = own[XCUT:].astype(jnp.bfloat16)

    def down_sum(dz):
        own = own2[dz, 2]
        x2send[dz, 1, :XCUT, :] = own[:XCUT].astype(jnp.bfloat16)
        x2send[dz, 1, XCUT:, :] = (own[XCUT:] + wide(rrecv[dz, XCUT:, :])).astype(jnp.bfloat16)

    def x_sum(dz):
        return own2[dz, 0] + wide(x2recv[dz, 0]) + wide(x2recv[dz, 1])

    def other_half():
        z2send[...] = x_sum(1).astype(jnp.bfloat16)

    def finish_high():
        mixed[high, :] = (x_sum(0) + wide(z2recv[...])).astype(jnp.bfloat16)

    def finish_low():
        total = own1[0] + wide(zrecv[0]) + wide(x1recv[0]) + wide(x1recv[1])
        mixed[low, :] = total.astype(jnp.bfloat16)

    def decode():
        for s in range(2):
            its, second = place(needs["block_of"][s] >> 1), (needs["block_of"][s] & 1) == 1
            for buf, at in ((kbuf, 0), (vbuf, HD)):
                block = buf[its]
                cache[s, :, at:at + HD] = jnp.where(second, block[SPAN // 2:], block[:SPAN // 2])

    steps = {
        "pvA": lambda: attend(low), "pvB": lambda: attend(high), "cache": decode,
        "q": other_half, "fl": finish_high, "fh": finish_low,
    }
    routes = {
        "z2": (z2send, z2recv, z_pair),
        "t2a": (tsend.at[pl.ds(0, ZCUT)], trecv.at[pl.ds(0, ZCUT)], x_up),
        "t2b": (
            tsend.at[pl.ds(ZCUT, ZROWS - ZCUT)], trecv.at[pl.ds(ZCUT, ZROWS - ZCUT)], x_down
        ),
        "x11": (x1send.at[0], x1recv.at[0], x_up),
        "x13": (x1send.at[1], x1recv.at[1], x_down),
    }
    for dx in range(4):
        routes[f"z1{dx}"] = (zsend.at[dx], zrecv.at[dx], z_pair)
        for dz in range(2):
            steps[f"A{dx}{dz}"] = functools.partial(low_term, dx, dz)
            steps[f"B{dx}{dz}"] = functools.partial(high_term, dx, dz)
    for dx in (1, 2, 3):
        steps[f"p{dx}"] = functools.partial(pair_sum, dx)
    for dz in range(2):
        steps[f"ea{dz}"] = functools.partial(up_sum, dz)
        steps[f"eb{dz}"] = functools.partial(down_sum, dz)
        for name, start, count, device in (
            (f"r{dz}a", 0, XCUT, x_up), (f"r{dz}b", XCUT, XROWS - XCUT, x_down)
        ):
            rows = pl.ds(start, count)
            routes[name] = (rsend.at[dz, rows], rrecv.at[dz, rows], device)
        routes[f"x21{dz}"] = (x2send.at[dz, 0], x2recv.at[dz, 0], x_up)
        routes[f"x23{dz}"] = (x2send.at[dz, 1], x2recv.at[dz, 1], x_down)
    for step in SUM_PLAN:
        name = step[1:]
        if step[0] == "+":
            copies[name] = send(*routes[name])
        elif step[0] == "?":
            arrive(name)
        else:
            steps[name]()

    for copy in sent:
        copy.wait_send()


def on_device(queries, key_values, out_weight, prompt_of, cycle_rank, span_len, cache_slot):
    bf16, f32 = jnp.bfloat16, jnp.float32
    width = HEADS * HD
    vmem = pltpu.VMEM
    return pl.pallas_call(
        kernel,
        out_shape=(
            vmem((SPAN, CHUNK), bf16),
            vmem((2, SPAN // 2, 2 * HD), bf16),
        ),
        in_specs=[pl.BlockSpec(memory_space=pl.ANY)] * 7,
        out_specs=(pl.BlockSpec(memory_space=pltpu.VMEM),) * 2,
        scratch_shapes=[
            vmem((SPAN, width), bf16),
            vmem((32, SPAN, HD), bf16),
            vmem((32, SPAN, HD), bf16),
            vmem((8, width, CHUNK), bf16),
            vmem((KEYS, 2 * HD), bf16),
            vmem((KEYS, HD), bf16),
            vmem((HEADS, SPAN, KEYS), bf16),
            vmem((HEADS, SPAN, HD), f32),
            vmem((SPAN, width), bf16),
            vmem((4, ZROWS, CHUNK), bf16),
            vmem((4, ZROWS, CHUNK), bf16),
            vmem((4, ZROWS, CHUNK), f32),
            vmem((ZROWS, CHUNK), bf16),
            vmem((ZROWS, CHUNK), bf16),
            vmem((2, ZROWS, CHUNK), bf16),
            vmem((2, ZROWS, CHUNK), bf16),
            vmem((2, XROWS, CHUNK), bf16),
            vmem((2, XROWS, CHUNK), bf16),
            vmem((2, 3, XROWS, CHUNK), f32),
            vmem((2, 2, XROWS, CHUNK), bf16),
            vmem((2, 2, XROWS, CHUNK), bf16),
            vmem((XROWS, CHUNK), bf16),
            vmem((XROWS, CHUNK), bf16),
            pltpu.SMEM((32,), jnp.int32),
            pltpu.SMEM((32,), jnp.int32),
            pltpu.SMEM((32,), jnp.int32),
            pltpu.SMEM((64,), jnp.int32),
            pltpu.SemaphoreType.DMA((24,)),
            pltpu.SemaphoreType.DMA((COPIES,)),
            pltpu.SemaphoreType.DMA((COPIES,)),
        ],
        compiler_params=pltpu.CompilerParams(
            collective_id=0, has_side_effects=True, vmem_limit_bytes=56 * 1024 * 1024
        ),
        cost_estimate=pl.CostEstimate(
            flops=4 * SPAN * HEADS * KEYS * HD + 2 * SPAN * width * 4096,
            bytes_accessed=10 * 1024 * 1024,
            transcendentals=HEADS * SPAN * KEYS,
        ),
    )(queries, key_values, out_weight, prompt_of, cycle_rank, span_len, cache_slot)


def solution(mesh):
    placed = (P("inst", "tp"), P("inst", "tp"), P("tp", None), P(), P(), P(), P())
    return jax.shard_map(
        on_device,
        mesh=mesh,
        in_specs=placed,
        out_specs=(P("inst", "tp"), P("inst", None, "tp")),
        check_vma=False,
    )
```

```python
import functools
import math

import jax
import jax.numpy as jnp
from jax import lax
from jax.experimental import pallas as pl
from jax.experimental.pallas import tpu as pltpu
from jax.sharding import PartitionSpec as P

HD = 128
SPAN = 256
HEADS = 8
EARLIER = 6
KEYS = (EARLIER + 1) * SPAN
CHUNK = 512
ZROWS = 112
XROWS = SPAN - ZROWS
ZCUT, XCUT = 48, 64
PART = SPAN
NEG = -1e30
MESH = pl.DeviceIdType.MESH
COPIES = 128
PIECES = ((0, 0, 128), (0, 128, 128), (1, 0, 128), (1, 128, 128))
SIBLING_FAR = 4

PLAN = (
    10003, 14300, 10103, 10101, 10203, 15200, 15100, 15300, 15000, 14000, 10001, 14200, 19100,
    14100, 10301, 25200, 17200, 24300, 16300, 25100, 17100, 24000, 16000, 20003, 11002, 20101,
    15003, 12102, 10201, 14101, 14003, 15101, 20001, 20103, 10303, 14001, 15103, 15001, 14103,
    20203, 20301, 11202, 15203, 14203, 15301, 12302, 27100, 14301, 21002, 15002, 22102, 14102,
    15102, 25001, 14002, 25000, 26300, 25101, 20201, 15201, 24103, 19200, 20303, 24001, 16103,
    16001, 14201, 15303, 21202, 26000, 22302, 14202, 15302, 24100, 19201, 17101, 24003, 24102,
    16102, 25102, 25301, 24200, 19000, 19300, 14303, 19101, 25300, 25003, 24301, 16301, 25103,
    24203, 17003, 25002, 29100, 19301, 16203, 24002, 17002, 19104, 15202, 25303, 19001, 29201,
    24101, 17303, 25302, 19304, 14302, 26001, 26103, 17302, 25201, 0, 27101, 27200, 24202, 19012,
    19112, 17201, 19004, 26102, 16202, 19108, 25203, 29301, 27003, 27002, 19008, 29200, 24201,
    19212, 29012, 29000, 29304, 29001, 24302, 29300, 27302, 26301, 26203, 27303, 25202, 29004,
    24303, 19204, 29112, 29108, 29104, 29101, 19312, 19308, 29008, 1, 27201, 26202, 19208, 1, 1, 1,
    1, 1, 1, 1, 29308, 29204, 29212, 29208, 29312,
)

SUM_PLAN = (
    "!pvB", "!B21", "+r1b", "+r1a", "!pvA", "!A21", "+z12", "!B20", "+r0b", "!B10", "!B30", "!B31",
    "+r0a", "!A01", "!B11", "!A11", "+z11", "!A31", "?r1a", "!ea1", "+x211", "+z13", "?r1b",
    "!eb1", "+x231", "!A20", "?z12", "!p2", "!B01", "?r0b", "+t2a", "!eb0", "?r0a", "!A10", "!A30",
    "+t2b", "!ea0", "+x230", "+x210", "+z10", "!B00", "?x231", "?x211", "!q", "?t2a", "!A00",
    "+z2", "?z11", "?t2b", "!p1", "?z13", "+x11", "!p3", "+x13", "?x210", "!cache", "?x11", "?z10",
    "?x230", "?z2", "!fl", "?x13", "!fh",
)


def kernel(
    q_hbm, kv_hbm, w_hbm, prompt_hbm, rank_hbm, len_hbm, slot_hbm,
    mixed, cache,
    qbuf, kbuf, vbuf, wbuf, kcat, vcat, probs, totals, att,
    zsend, zrecv, own1, tsend, trecv, x1send, x1recv,
    rsend, rrecv, own2, x2send, x2recv, z2send, z2recv,
    prompt, rank, length, slot,
    local_sem, send_sem, recv_sem,
):
    me = lax.axis_index("inst")
    tp = lax.axis_index("tp")
    y, zh, core = me // 8, (me // 2) % 4, me % 2
    x, zl = tp // 2, tp % 2

    def inst_at(dy, dz, dc):
        return (((y + dy) % 4) * 4 + (zh + dz) % 4) * 2 + (core + dc) % 2

    def tp_at(dx, dz):
        return ((x + dx) % 4) * 2 + (zl + dz) % 2

    z_up, z_down = (inst_at(0, 1, 0), tp), (inst_at(0, 3, 0), tp)
    z_across, y_across = (inst_at(0, 2, 0), tp), (inst_at(2, 0, 0), tp)
    y_up, y_down = (inst_at(1, 0, 0), tp), (inst_at(3, 0, 0), tp)
    sibling = (inst_at(0, 0, 1), tp)
    z_pair = (me, tp_at(0, 1))
    x_up, x_down = (me, tp_at(1, 0)), (me, tp_at(3, 0))

    barrier = pltpu.get_barrier_semaphore()
    friends = [z_up, z_down, y_up, y_down, sibling, z_pair, x_up, x_down]
    for friend in friends:
        pl.semaphore_signal(barrier, inc=1, device_id=friend, device_id_type=MESH)

    n_local = [0]

    def local(src, dst):
        copy = pltpu.make_async_copy(src, dst, local_sem.at[n_local[0]])
        n_local[0] += 1
        copy.start()
        return copy

    own_k = local(kv_hbm.at[:, pl.ds(0, HD)], kbuf.at[0])
    own_v = local(kv_hbm.at[:, pl.ds(HD, HD)], vbuf.at[0])
    tables = [
        local(src, dst)
        for src, dst in (
            (prompt_hbm, prompt), (rank_hbm, rank), (len_hbm, length), (slot_hbm, slot)
        )
    ]
    w_copies, q_copies = {}, []

    def start_large():
        q_copies.append(local(q_hbm, qbuf))
        for dz in (1, 0):
            for dx in (2, 1, 3, 0):
                columns = pl.ds(pl.multiple_of(tp_at(dx, dz) * CHUNK, CHUNK), CHUNK)
                w_copies[dx, dz] = local(w_hbm.at[:, columns], wbuf.at[dx * 2 + dz])

    pl.semaphore_wait(barrier, len(friends))

    sent = []

    def send(src, dst, device):
        index = len(sent)
        copy = pltpu.make_async_remote_copy(
            src_ref=src, dst_ref=dst, send_sem=send_sem.at[index], recv_sem=recv_sem.at[index],
            device_id=device, device_id_type=MESH,
        )
        copy.start()
        sent.append(copy)
        return copy

    copies = {}

    def start_copy(code):
        kind, piece, at = code // 1000, code // 100 % 10, code % 100
        which, first_row, rows = PIECES[piece]
        source, target, device = (
            (0, at, z_up if at == 3 else z_down),
            (3, at, z_up), (1, at, z_down), (0, at, z_across),
            (at, 12 + at, y_up), (at, 4 + at, y_down),
            (12 + at, 8 + at, y_up), (4 + at, 8 + at, y_down), (at, 8 + at, y_across),
            (at, 16 + at, sibling),
        )[kind]
        count = {0: 1, 1: 3, 4: 4, 12: 4, 8: SIBLING_FAR, 10: 2}[at] if kind == 9 else 1
        buf, piece_rows = (kbuf, vbuf)[which], pl.ds(first_row, rows)
        copies[code] = send(
            buf.at[pl.ds(source, count), piece_rows], buf.at[pl.ds(target, count), piece_rows], device
        )

    arrived = set()

    def arrive(name):
        if name not in arrived:
            arrived.add(name)
            copies[name].wait_recv()

    own_k.wait()
    own_v.wait()
    needs = {}

    def look_up():
        for copy in tables:
            copy.wait()
        my_prompt, my_rank, my_len = prompt[me], rank[me], length[me]
        who, live = [me] * EARLIER, [jnp.int32(0)] * EARLIER
        for j in range(32):
            same, its_rank, its_len = prompt[j] == my_prompt, rank[j], length[j]
            for s in range(EARLIER):
                hit = same & (its_rank == s) & (s < my_rank)
                who[s] = jnp.where(hit, j, who[s])
                live[s] = jnp.where(hit, its_len, live[s])
        block_of = [jnp.int32(0)] * 2
        for b in range(64):
            for s in range(2):
                block_of[s] = jnp.where(slot[b] == 2 * me + s, b, block_of[s])
        needs.update(who=who, block_of=block_of, my_len=my_len)
        key_row = lax.broadcasted_iota(jnp.int32, (SPAN, HD), 0)
        first_lane = lax.broadcasted_iota(jnp.int32, (SPAN, HD), 1) == 0
        for s in range(EARLIER):
            dead = first_lane & (key_row >= live[s])
            kcat[s * SPAN:(s + 1) * SPAN, HD:] = jnp.where(dead, NEG, 0.0).astype(jnp.bfloat16)
        kcat[EARLIER * SPAN:, HD:] = jnp.zeros((SPAN, HD), jnp.bfloat16)

    def place(j):
        dy = ((j >> 3) + 4 - y) & 3
        dz = (((j >> 1) & 3) + 4 - zh) & 3
        dc = ((j & 1) + 2 - core) & 1
        return dc * 16 + dy * 4 + dz

    def take_keys():
        q_copies[0].wait()
        for s in range(EARLIER):
            kcat[s * SPAN:(s + 1) * SPAN, :HD] = kbuf[place(needs["who"][s])]
        kcat[EARLIER * SPAN:, :HD] = kbuf[0]

    factor = math.log2(math.e) / math.sqrt(HD)

    ones = (lax.broadcasted_iota(jnp.int32, (PART, HD), 1) == 0).astype(jnp.bfloat16)

    def weigh(head, start):
        rows = slice(start, start + PART)
        query = qbuf[rows, head * HD:(head + 1) * HD]
        scores = lax.dot_general(
            jnp.concatenate([query, ones], axis=1), kcat[...],
            (((1,), (1,)), ((), ())), preferred_element_type=jnp.float32,
        )
        earlier = scores[:, :EARLIER * SPAN]
        row = lax.broadcasted_iota(jnp.int32, (PART, SPAN), 0) + start
        column = lax.broadcasted_iota(jnp.int32, (PART, SPAN), 1)
        here = jnp.where(column <= row, scores[:, EARLIER * SPAN:], NEG)
        top = jnp.maximum(
            jnp.max(earlier, axis=1, keepdims=True), jnp.max(here, axis=1, keepdims=True)
        )
        earlier = jnp.exp2((earlier - top) * factor)
        here = jnp.exp2((here - top) * factor)
        total = jnp.sum(earlier, axis=1, keepdims=True) + jnp.sum(here, axis=1, keepdims=True)
        its_row = lax.broadcasted_iota(jnp.int32, (PART, 1), 0) + start
        inverse = jnp.where(its_row < needs["my_len"], 1.0 / total, 0.0)
        probs[head, rows, :EARLIER * SPAN] = earlier.astype(jnp.bfloat16)
        probs[head, rows, EARLIER * SPAN:] = here.astype(jnp.bfloat16)
        totals[head, rows, :] = jnp.broadcast_to(inverse, (PART, HD))

    weighed = 0
    for step in PLAN:
        if step >= 20000 and not q_copies:
            start_large()
        if step == 0:
            look_up()
        elif step == 1:
            if not weighed:
                take_keys()
            weigh(weighed, 0)
            weighed += 1
        elif step < 20000:
            start_copy(step - 10000)
        else:
            arrive(step - 20000)
    for name in copies:
        arrive(name)

    for s in range(EARLIER):
        vcat[s * SPAN:(s + 1) * SPAN, :] = vbuf[place(needs["who"][s])]
    vcat[EARLIER * SPAN:, :] = vbuf[0]

    def attend(rows):
        for head in range(HEADS):
            numer = jnp.dot(probs[head, rows, :], vcat[...], preferred_element_type=jnp.float32)
            attended = numer * totals[head, rows, :]
            att[rows, head * HD:(head + 1) * HD] = attended.astype(jnp.bfloat16)

    low, high = slice(0, ZROWS), slice(ZROWS, SPAN)
    ready = set()

    def project(rows, dx, dz):
        if (dx, dz) not in ready:
            ready.add((dx, dz))
            w_copies[dx, dz].wait()
        return jnp.dot(att[rows, :], wbuf[dx * 2 + dz], preferred_element_type=jnp.float32)

    def low_term(dx, dz):
        if dz:
            zsend[dx] = project(low, dx, dz).astype(jnp.bfloat16)
        else:
            own1[dx] = project(low, dx, dz)

    def high_term(dx, dz):
        if dx == 2:
            rsend[dz] = project(high, dx, dz).astype(jnp.bfloat16)
        else:
            own2[dz, {0: 0, 1: 1, 3: 2}[dx]] = project(high, dx, dz)

    def wide(values):
        return values.astype(jnp.float32)

    def pair_sum(dx):
        total = own1[dx] + wide(zrecv[dx])
        if dx == 2:
            tsend[...] = total.astype(jnp.bfloat16)
        elif dx == 1:
            x1send[0, :ZCUT, :] = (total[:ZCUT] + wide(trecv[:ZCUT, :])).astype(jnp.bfloat16)
            x1send[0, ZCUT:, :] = total[ZCUT:].astype(jnp.bfloat16)
        else:
            x1send[1, :ZCUT, :] = total[:ZCUT].astype(jnp.bfloat16)
            x1send[1, ZCUT:, :] = (total[ZCUT:] + wide(trecv[ZCUT:, :])).astype(jnp.bfloat16)

    def up_sum(dz):
        own = own2[dz, 1]
        x2send[dz, 0, :XCUT, :] = (own[:XCUT] + wide(rrecv[dz, :XCUT, :])).astype(jnp.bfloat16)
        x2send[dz, 0, XCUT:, :] = own[XCUT:].astype(jnp.bfloat16)

    def down_sum(dz):
        own = own2[dz, 2]
        x2send[dz, 1, :XCUT, :] = own[:XCUT].astype(jnp.bfloat16)
        x2send[dz, 1, XCUT:, :] = (own[XCUT:] + wide(rrecv[dz, XCUT:, :])).astype(jnp.bfloat16)

    def x_sum(dz):
        return own2[dz, 0] + wide(x2recv[dz, 0]) + wide(x2recv[dz, 1])

    def other_half():
        z2send[...] = x_sum(1).astype(jnp.bfloat16)

    def finish_high():
        mixed[high, :] = (x_sum(0) + wide(z2recv[...])).astype(jnp.bfloat16)

    def finish_low():
        total = own1[0] + wide(zrecv[0]) + wide(x1recv[0]) + wide(x1recv[1])
        mixed[low, :] = total.astype(jnp.bfloat16)

    def decode():
        for s in range(2):
            its, second = place(needs["block_of"][s] >> 1), (needs["block_of"][s] & 1) == 1
            for buf, at in ((kbuf, 0), (vbuf, HD)):
                block = buf[its]
                cache[s, :, at:at + HD] = jnp.where(second, block[SPAN // 2:], block[:SPAN // 2])

    steps = {
        "pvA": lambda: attend(low), "pvB": lambda: attend(high), "cache": decode,
        "q": other_half, "fl": finish_high, "fh": finish_low,
    }
    routes = {
        "z2": (z2send, z2recv, z_pair),
        "t2a": (tsend.at[pl.ds(0, ZCUT)], trecv.at[pl.ds(0, ZCUT)], x_up),
        "t2b": (
            tsend.at[pl.ds(ZCUT, ZROWS - ZCUT)], trecv.at[pl.ds(ZCUT, ZROWS - ZCUT)], x_down
        ),
        "x11": (x1send.at[0], x1recv.at[0], x_up),
        "x13": (x1send.at[1], x1recv.at[1], x_down),
    }
    for dx in range(4):
        routes[f"z1{dx}"] = (zsend.at[dx], zrecv.at[dx], z_pair)
        for dz in range(2):
            steps[f"A{dx}{dz}"] = functools.partial(low_term, dx, dz)
            steps[f"B{dx}{dz}"] = functools.partial(high_term, dx, dz)
    for dx in (1, 2, 3):
        steps[f"p{dx}"] = functools.partial(pair_sum, dx)
    for dz in range(2):
        steps[f"ea{dz}"] = functools.partial(up_sum, dz)
        steps[f"eb{dz}"] = functools.partial(down_sum, dz)
        for name, start, count, device in (
            (f"r{dz}a", 0, XCUT, x_up), (f"r{dz}b", XCUT, XROWS - XCUT, x_down)
        ):
            rows = pl.ds(start, count)
            routes[name] = (rsend.at[dz, rows], rrecv.at[dz, rows], device)
        routes[f"x21{dz}"] = (x2send.at[dz, 0], x2recv.at[dz, 0], x_up)
        routes[f"x23{dz}"] = (x2send.at[dz, 1], x2recv.at[dz, 1], x_down)
    for step in SUM_PLAN:
        name = step[1:]
        if step[0] == "+":
            copies[name] = send(*routes[name])
        elif step[0] == "?":
            arrive(name)
        else:
            steps[name]()

    for copy in sent:
        copy.wait_send()


def on_device(queries, key_values, out_weight, prompt_of, cycle_rank, span_len, cache_slot):
    bf16, f32 = jnp.bfloat16, jnp.float32
    width = HEADS * HD
    vmem = pltpu.VMEM
    return pl.pallas_call(
        kernel,
        out_shape=(
            vmem((SPAN, CHUNK), bf16),
            vmem((2, SPAN // 2, 2 * HD), bf16),
        ),
        in_specs=[pl.BlockSpec(memory_space=pl.ANY)] * 7,
        out_specs=(pl.BlockSpec(memory_space=pltpu.VMEM),) * 2,
        scratch_shapes=[
            vmem((SPAN, width), bf16),
            vmem((32, SPAN, HD), bf16),
            vmem((32, SPAN, HD), bf16),
            vmem((8, width, CHUNK), bf16),
            vmem((KEYS, 2 * HD), bf16),
            vmem((KEYS, HD), bf16),
            vmem((HEADS, SPAN, KEYS), bf16),
            vmem((HEADS, SPAN, HD), f32),
            vmem((SPAN, width), bf16),
            vmem((4, ZROWS, CHUNK), bf16),
            vmem((4, ZROWS, CHUNK), bf16),
            vmem((4, ZROWS, CHUNK), f32),
            vmem((ZROWS, CHUNK), bf16),
            vmem((ZROWS, CHUNK), bf16),
            vmem((2, ZROWS, CHUNK), bf16),
            vmem((2, ZROWS, CHUNK), bf16),
            vmem((2, XROWS, CHUNK), bf16),
            vmem((2, XROWS, CHUNK), bf16),
            vmem((2, 3, XROWS, CHUNK), f32),
            vmem((2, 2, XROWS, CHUNK), bf16),
            vmem((2, 2, XROWS, CHUNK), bf16),
            vmem((XROWS, CHUNK), bf16),
            vmem((XROWS, CHUNK), bf16),
            pltpu.SMEM((32,), jnp.int32),
            pltpu.SMEM((32,), jnp.int32),
            pltpu.SMEM((32,), jnp.int32),
            pltpu.SMEM((64,), jnp.int32),
            pltpu.SemaphoreType.DMA((24,)),
            pltpu.SemaphoreType.DMA((COPIES,)),
            pltpu.SemaphoreType.DMA((COPIES,)),
        ],
        compiler_params=pltpu.CompilerParams(
            collective_id=0, has_side_effects=True, vmem_limit_bytes=56 * 1024 * 1024
        ),
        cost_estimate=pl.CostEstimate(
            flops=4 * SPAN * HEADS * KEYS * HD + 2 * SPAN * width * 4096,
            bytes_accessed=10 * 1024 * 1024,
            transcendentals=HEADS * SPAN * KEYS,
        ),
    )(queries, key_values, out_weight, prompt_of, cycle_rank, span_len, cache_slot)


def solution(mesh):
    placed = (P("inst", "tp"), P("inst", "tp"), P("tp", None), P(), P(), P(), P())
    return jax.shard_map(
        on_device,
        mesh=mesh,
        in_specs=placed,
        out_specs=(P("inst", "tp"), P("inst", None, "tp")),
        check_vma=False,
    )
```
